32 devices in a mesh: rows: 8 (over y, x, core), grp: 4 (over z).
Axes of the slice: x: 2, y: 2, z: 4, core: 2. Of those that a mesh axis runs over, the one named last changes fastest.
Arguments:
- vector: float32 [128, 16, 384], P(('rows', 'grp')), may hold values from -20 to 20
- near_cols: int32 [128, 3], P(('rows', 'grp')), may hold values from 0 to 127, as said below
- near_blocks: bfloat16 [128, 3, 384, 384], P(('rows', 'grp')), may hold values from -2 to 2
- col_basis: bfloat16 [128, 32, 384], P(('rows', 'grp')), may hold values from -0.3125 to 0.3125
- row_basis: bfloat16 [128, 32, 384], P(('rows', 'grp')), may hold values from -1 to 1
- leaf_far: int32 [128, 8], P(('rows', 'grp')), may hold values from 0 to 127, as said below
- leaf_coupling: bfloat16 [128, 32, 256], P(('rows', 'grp')), may hold values from -0.375 to 0.375
- leaf_transfer: float32 [128, 32, 32], P(('rows', 'grp')), may hold values from -0.5 to 0.5
- box_far: int32 [32, 4], P(('rows', 'grp')), may hold values from 0 to 31, as said below
- box_coupling: bfloat16 [32, 32, 128], P(('rows', 'grp')), may hold values from -0.5 to 0.5
- box_transfer: float32 [32, 32, 32], P(('rows', 'grp')), may hold values from -1 to 1
- coarse_far: int32 [8, 4], P('rows'), may hold values from 0 to 7, as said below
- coarse_coupling: bfloat16 [8, 32, 128], P('rows'), may hold values from -0.5 to 0.5
Outputs:
- basis: float32 [128, 16, 384], P(('rows', 'grp'))
- remainder: float32 [128, 16, 384], P(('rows', 'grp'))
- hessenberg: float32 [16, 5], replicated
The draws below stay inside these ranges and needn't reach their ends.
Inputs may be any that keep to these rules, and one draw needn't show every extreme that they name: `near_cols`: entry 0 of leaf l is l itself; the other entries are distinct leaves l + o with 0 < |o| <= 4. `leaf_far`: the entries of leaf l are distinct leaves g with |g - l| > 4 and |g // 16 - l // 16| <= 1. `box_far`: the entries of box x are distinct boxes y with |y - x| > 1 and |y // 4 - x // 4| <= 1. `coarse_far`: the entries of group g are distinct groups h with |h - g| > 1.
All inputs are finite; a program needn't handle non-finite values.
Results may differ from the reference program's by a relative error of at most 0.015.
Values may be sent and summed in bfloat16 or wider, within the bound.
A program may use at most 64 MiB of HBM per device.

```python
import jax
import jax.numpy as jnp
from jax import lax

LP = 128
R = 32
NRHS = 16
LD = 4
KN = 3
KF = 8
KB = 4
KC = 4
BOX_GROUP = 4
GROUPS = 8
BOXES = 32
LEAVES = 128
GL = 16


def pick_distinct(key, candidates, valid, count):
    total_rows, span = candidates.shape
    offsets = jnp.arange(span, dtype=jnp.int32)[None, :]
    raw_scores = jax.random.randint(key, (total_rows, span), 0, 1 << 16, dtype=jnp.int32)
    scores = jnp.where(valid, raw_scores * span + offsets, -1 - offsets)
    picked_values, picked = lax.top_k(scores, count)
    return jnp.take_along_axis(candidates, picked, axis=1).astype(jnp.int32)


def draw_vector(key, part):
    key_base, key_rough = jax.random.split(jax.random.fold_in(key, 11))
    shape = (LEAVES, NRHS, 3 * LP)
    ramp = jnp.arange(LEAVES, dtype=jnp.float32)[:, None, None] / max(LEAVES - 1, 1)
    rough = jnp.exp(jax.random.uniform(key_rough, (LEAVES, NRHS, 1), jnp.float32, -0.35, 0.35))
    base = jax.random.truncated_normal(key_base, -4.0, 4.0, shape, jnp.float32)
    scale = 1.0 + 2.0 * ramp
    return (base * scale * rough).astype(jnp.float32)


def draw_near_blocks(key, part):
    base_key = jax.random.fold_in(key, 61)
    width = 3 * LP

    def one_leaf(leaf):
        key_self, key_rest = jax.random.split(jax.random.fold_in(base_key, leaf))
        raw_self = jax.random.truncated_normal(key_self, -4.0, 4.0, (width, width), jnp.float32)
        raw_rest = jax.random.truncated_normal(key_rest, -4.0, 4.0, (KN - 1, width, width), jnp.float32)
        own_block = (raw_self + raw_self.T) * (1.5 / (2.0 * width) ** 0.5)
        other_blocks = raw_rest / (width * KN) ** 0.5
        return jnp.concatenate([own_block[None], other_blocks], axis=0).astype(jnp.bfloat16)
    return lax.map(one_leaf, jnp.arange(LEAVES, dtype=jnp.int32))


def draw_near_cols(key, part):
    leaf = jnp.arange(LEAVES, dtype=jnp.int32)[:, None]
    offsets = jnp.concatenate([jnp.arange(-LD, 0, dtype=jnp.int32), jnp.arange(1, LD + 1, dtype=jnp.int32)])[None, :]
    candidates = leaf + offsets
    valid = (candidates >= 0) & (candidates < LEAVES)
    others = pick_distinct(jax.random.fold_in(key, 21), candidates, valid, KN - 1)
    return jnp.concatenate([leaf, others], axis=1).astype(jnp.int32)


def draw_leaf_far(key, part):
    leaf = jnp.arange(LEAVES, dtype=jnp.int32)[:, None]
    slots = jnp.arange(3 * GL, dtype=jnp.int32)[None, :]
    candidates = (leaf // GL - 1) * GL + slots
    valid = (candidates >= 0) & (candidates < LEAVES) & (jnp.abs(candidates - leaf) > LD)
    return pick_distinct(jax.random.fold_in(key, 31), candidates, valid, KF)


def draw_box_far(key, part):
    box_index = jnp.arange(BOXES, dtype=jnp.int32)[:, None]
    slots = jnp.arange(3 * BOX_GROUP, dtype=jnp.int32)[None, :]
    candidates = (box_index // BOX_GROUP - 1) * BOX_GROUP + slots
    valid = (candidates >= 0) & (candidates < BOXES) & (jnp.abs(candidates - box_index) > 1)
    return pick_distinct(jax.random.fold_in(key, 41), candidates, valid, KB)


def draw_coarse_far(key, part):
    group_index = jnp.arange(GROUPS, dtype=jnp.int32)[:, None]
    candidates = jnp.broadcast_to(jnp.arange(GROUPS, dtype=jnp.int32)[None, :], (GROUPS, GROUPS))
    valid = jnp.abs(candidates - group_index) > 1
    return pick_distinct(jax.random.fold_in(key, 51), candidates, valid, KC)


def block_levels(stream_key, shape, cuts, least, top_value):
    gain = 1.0
    for dim, parts in cuts:
        steps = jax.random.uniform(jax.random.fold_in(jax.random.fold_in(stream_key, 6), dim), (parts,), jnp.float32, least / len(cuts), top_value / len(cuts))
        gain = gain * jnp.repeat(jnp.exp(steps), shape[dim] // parts).reshape((-1,) + (1,) * (len(shape) - 1 - dim))
    return gain


def noise(own_key, extent, scale, bound, cuts=(), kind=jnp.bfloat16):
    entries = scale * jax.random.normal(own_key, extent, jnp.float32)
    if cuts:
        entries = entries * block_levels(own_key, extent, cuts, -0.22, 0.18)
    return jnp.clip(entries, -bound, bound).astype(kind)


def setup_inputs(seed: int = 0) -> dict:
    arg_keys = jax.random.split(jax.random.key(seed), 14)
    vector = draw_vector(jax.random.fold_in(arg_keys[13], 71), 0)
    near_cols = draw_near_cols(jax.random.fold_in(arg_keys[13], 71), 0)
    near_blocks = draw_near_blocks(jax.random.fold_in(arg_keys[13], 71), 0)
    col_basis = noise(arg_keys[3], (LEAVES, R, 3 * LP), (3 * LP) ** -0.5, 0.3125, ((0, 32),))
    row_basis = noise(arg_keys[4], (LEAVES, R, 3 * LP), R ** -0.5, 1.0, ((0, 32),))
    leaf_far = draw_leaf_far(jax.random.fold_in(arg_keys[13], 71), 0)
    leaf_coupling = noise(arg_keys[6], (LEAVES, R, KF * R), (KF * R) ** -0.5, 0.375, ((0, 32),))
    leaf_transfer = noise(arg_keys[7], (LEAVES, R, R), (LD * R) ** -0.5, 0.5, ((0, 32),), jnp.float32)
    box_far = draw_box_far(jax.random.fold_in(arg_keys[13], 71), 0)
    box_coupling = noise(arg_keys[9], (BOXES, R, KB * R), (KB * R) ** -0.5, 0.5, ((0, 32),))
    box_transfer = noise(arg_keys[10], (BOXES, R, R), R ** -0.5, 1.0, ((0, 32),), jnp.float32)
    coarse_far = draw_coarse_far(jax.random.fold_in(arg_keys[13], 71), 0)
    coarse_coupling = noise(arg_keys[12], (GROUPS, R, KC * R), (KC * R) ** -0.5, 0.5, ((0, 8),))
    return {"vector": vector, "near_cols": near_cols, "near_blocks": near_blocks, "col_basis": col_basis, "row_basis": row_basis, "leaf_far": leaf_far, "leaf_coupling": leaf_coupling, "leaf_transfer": leaf_transfer, "box_far": box_far, "box_coupling": box_coupling, "box_transfer": box_transfer, "coarse_far": coarse_far, "coarse_coupling": coarse_coupling}


highest = lax.Precision.HIGHEST
epsilon = 1e-06

def to_float(array):
    return array.astype(jnp.float32)

def near_term(field_bf, near_cols, near_blocks):
    columns = near_cols.reshape(BOXES, LD, KN)
    blocks = near_blocks.reshape(BOXES, LD, KN, 3 * LP, 3 * LP)

    def per_box(operands):
        picked = to_float(jnp.take(field_bf, operands[0], axis=0))
        return jnp.einsum('lkbj,lkij->lbi', picked, to_float(operands[1]))
    return lax.map(per_box, (columns, blocks)).reshape(LEAVES, NRHS, 3 * LP)

def gather_flat(source, indices):
    chosen = jnp.take(source, indices, axis=0)
    chosen = jnp.transpose(chosen, (0, 2, 1, 3))
    return chosen.reshape(indices.shape[0], NRHS, indices.shape[1] * R)

def apply_operator(field, near_cols, near_blocks, col_basis, row_basis, leaf_far, leaf_coupling, leaf_transfer, box_far, box_coupling, box_transfer, coarse_far, coarse_coupling):
    field_bf = field.astype(jnp.bfloat16)
    near_sum = near_term(field_bf, near_cols, near_blocks)
    leaf_coef = jnp.einsum('lbj,lrj->lbr', to_float(field_bf), to_float(col_basis)).astype(jnp.bfloat16)
    leaf_blocks = leaf_transfer.reshape(BOXES, LD, R, R)
    box_coef = jnp.einsum('xlbr,xlrs->xbs', to_float(leaf_coef).reshape(BOXES, LD, NRHS, R), leaf_blocks, precision=highest).astype(jnp.bfloat16)
    parent_part = jnp.einsum('xbr,xrs->xbs', to_float(box_coef), box_transfer, precision=highest).astype(jnp.bfloat16)
    group_coef = to_float(parent_part).reshape(GROUPS, BOX_GROUP, NRHS, R).sum(axis=1).astype(jnp.bfloat16)
    leaf_field = jnp.einsum('lbm,lrm->lbr', to_float(gather_flat(leaf_coef, leaf_far)), to_float(leaf_coupling))
    box_field = jnp.einsum('xbm,xrm->xbr', to_float(gather_flat(box_coef, box_far)), to_float(box_coupling))
    group_field = jnp.einsum('gbm,grm->gbr', to_float(gather_flat(group_coef, coarse_far)), to_float(coarse_coupling))
    spread = jnp.repeat(group_field, BOX_GROUP, axis=0)
    box_local = box_field + jnp.einsum('xbs,xrs->xbr', spread, box_transfer, precision=highest)
    leaf_local = leaf_field + jnp.einsum('xbs,xlrs->xlbr', box_local, leaf_blocks, precision=highest).reshape(LEAVES, NRHS, R)
    leaf_local = leaf_local.astype(jnp.bfloat16)
    far_sum = jnp.einsum('lbr,lrj->lbj', to_float(leaf_local), to_float(row_basis))
    return 0.5 * field + near_sum + far_sum

def mean_product(left, right):
    return lax.optimization_barrier(jnp.mean(left * right, axis=(0, 2)))

def spread_rhs(values):
    return values[None, :, None]

def reference(vector, near_cols, near_blocks, col_basis, row_basis, leaf_far, leaf_coupling, leaf_transfer, box_far, box_coupling, box_transfer, coarse_far, coarse_coupling):

    def operator(field):
        return apply_operator(field, near_cols, near_blocks, col_basis, row_basis, leaf_far, leaf_coupling, leaf_transfer, box_far, box_coupling, box_transfer, coarse_far, coarse_coupling)
    norm_first = jnp.sqrt(mean_product(vector, vector) + epsilon)
    first_basis = vector / spread_rhs(norm_first)
    image_one = operator(first_basis)
    proj_first = mean_product(first_basis, image_one)
    image_one = image_one - spread_rhs(proj_first) * first_basis
    norm_image = jnp.sqrt(mean_product(image_one, image_one) + epsilon)
    basis = image_one / spread_rhs(norm_image)
    remainder = operator(basis)
    proj_second = mean_product(first_basis, remainder)
    remainder = remainder - spread_rhs(proj_second) * first_basis
    proj_basis = mean_product(basis, remainder)
    remainder = remainder - spread_rhs(proj_basis) * basis
    norm_last = jnp.sqrt(mean_product(remainder, remainder) + epsilon)
    hessenberg = jnp.stack([proj_first, norm_image, proj_second, proj_basis, norm_last], axis=1)
    return (basis, remainder, hessenberg)
```

```python
import functools

import jax
import jax.numpy as jnp
from jax import lax
from jax.experimental import pallas as pl
from jax.experimental.pallas import tpu as pltpu
from jax.sharding import PartitionSpec as P

LANES = 128
epsilon = 1e-06
highest = lax.Precision.HIGHEST
MESH = pl.DeviceIdType.MESH
bf16 = jnp.bfloat16
f32 = jnp.float32


def nt(left, right, precision=None):
    return lax.dot_general(
        left, right, (((1,), (1,)), ((), ())), precision=precision, preferred_element_type=f32
    )


def spread_matrix(rows, slots, rank, low, copies):
    shape = (rows, slots * LANES)
    row = lax.broadcasted_iota(jnp.int32, shape, 0)
    column = lax.broadcasted_iota(jnp.int32, shape, 1)
    lane = column % LANES - low
    wanted = (column // LANES) * rank + lane % rank
    hit = (row == wanted) & (lane >= 0) & (lane < copies * rank)
    return jnp.where(hit, 1.0, 0.0).astype(bf16)


def kernel(
    rows,
    grp,
    *refs,
):
    sources = refs[:13]
    basis_out, remainder_out, hessenberg_out = refs[13:16]
    targets = refs[16:29]
    (
        near_cols,
        leaf_far,
        box_far,
        coarse_far,
        vector,
        near_blocks,
        col_basis,
        row_basis,
        leaf_coupling,
        leaf_transfer,
        box_coupling,
        box_transfer,
        coarse_coupling,
    ) = targets
    (
        field_a,
        field_b,
        coef_a,
        coef_b,
        group_a,
        group_b,
        sums_a,
        sums_b,
        send_basis,
        receive_basis,
        leaf_weights,
        box_weights,
        group_weights,
        image,
        image_two,
        load_sem,
        field_send,
        field_recv,
        coef_send,
        coef_recv,
        group_send,
        group_recv,
        sums_send,
        sums_recv,
    ) = refs[29:]
    leaves, rhs, cells = vector.shape
    rank = col_basis.shape[1]
    near_count = near_cols.shape[1]
    leaf_slots = leaf_far.shape[1]
    box_slots = box_far.shape[1]
    coarse_slots = coarse_far.shape[1]
    devices = rows * grp
    total_count = leaves * devices * cells
    row = lax.axis_index("rows")
    z = lax.axis_index("grp")
    me = row * grp + z

    loads = [
        pltpu.make_async_copy(source, target, load_sem.at[n])
        for n, (source, target) in enumerate(zip(sources, targets))
    ]
    for n in (4, 6, 9, 11, 7, 8, 10, 12, 0, 1, 2, 3, 5):
        loads[n].start()

    barrier = pltpu.get_barrier_semaphore()

    def greet(step, carry):
        other = lax.rem(me + step, devices)
        pl.semaphore_signal(
            barrier,
            inc=1,
            device_id=(lax.div(other, grp), lax.rem(other, grp)),
            device_id_type=MESH,
        )
        return carry

    lax.fori_loop(1, devices, greet, 0)

    send_basis[...] = jnp.zeros_like(send_basis)
    for n in (4, 6, 9, 11):
        loads[n].wait()
    for l in range(leaves):
        send_basis[l * rank : (l + 1) * rank, l * cells : (l + 1) * cells] = col_basis[l]
    width = leaves * rank
    transfer = leaf_transfer[...].reshape(width, rank)
    up_box = lax.dot_general(
        transfer,
        send_basis[:width].astype(f32),
        (((0,), (0,)), ((), ())),
        precision=highest,
        preferred_element_type=f32,
    )
    up_parent = lax.dot_general(
        box_transfer[0],
        up_box,
        (((0,), (0,)), ((), ())),
        precision=highest,
        preferred_element_type=f32,
    )
    send_basis[width : width + rank] = up_box.astype(bf16)
    send_basis[width + rank : width + 2 * rank] = up_parent.astype(bf16)

    def prepare_receive():
        for n in (7, 8, 10, 12, 0, 1, 2, 3):
            loads[n].wait()
        receive_basis[...] = jnp.zeros_like(receive_basis)
        for l in range(leaves):
            receive_basis[l * rank : (l + 1) * rank, l * cells : (l + 1) * cells] = row_basis[l]
        tiled = jnp.dot(
            leaf_coupling[...].reshape(width, leaf_slots * rank),
            spread_matrix(leaf_slots * rank, leaf_slots, rank, 0, leaves),
            preferred_element_type=f32,
        )
        part = lax.broadcasted_iota(jnp.int32, (rank, LANES), 1) // rank
        for l in range(leaves):
            for k in range(leaf_slots):
                sub = lax.rem(leaf_far[l, k], leaves)
                piece = tiled[l * rank : (l + 1) * rank, k * LANES : (k + 1) * LANES]
                leaf_weights[l, :, k * LANES : (k + 1) * LANES] = jnp.where(
                    part == sub, piece, 0.0
                ).astype(bf16)
        box_wide = jnp.dot(
            box_coupling[0],
            spread_matrix(box_slots * rank, box_slots, rank, 0, 1),
            preferred_element_type=f32,
        )
        box_weights[...] = jnp.dot(
            transfer, box_wide, precision=highest, preferred_element_type=f32
        ).astype(bf16)
        group_wide = jnp.dot(
            coarse_coupling[0],
            spread_matrix(coarse_slots * rank, coarse_slots, rank, rank, 1),
            preferred_element_type=f32,
        )
        down = jnp.dot(transfer, box_transfer[0], precision=highest, preferred_element_type=f32)
        group_weights[...] = jnp.dot(
            down, group_wide, precision=highest, preferred_element_type=f32
        ).astype(bf16)

    def send(src, dst, send_sem, recv_sem, to_row, to_z):
        pltpu.make_async_remote_copy(
            src_ref=src,
            dst_ref=dst,
            send_sem=send_sem,
            recv_sem=recv_sem,
            device_id=(to_row, to_z),
            device_id_type=MESH,
        ).start()

    def wait_bytes(ref, sem):
        pltpu.make_async_copy(ref, ref, sem).wait()

    def operator(phase, source, result, field, coef, group, after_send, before_near):
        for l in range(leaves):
            field[leaves + l] = source[l].astype(bf16)
        if phase == 0:
            pl.semaphore_wait(barrier, devices - 1)
        own = field.at[pl.ds(leaves, leaves)]
        low = field.at[pl.ds(0, leaves)]
        high = field.at[pl.ds(2 * leaves, leaves)]

        @pl.when(me < devices - 1)
        def _():
            other = me + 1
            send(
                own,
                low,
                field_send.at[phase, 0],
                field_recv.at[phase, 0],
                lax.div(other, grp),
                lax.rem(other, grp),
            )

        @pl.when(me > 0)
        def _():
            other = me - 1
            send(
                own,
                high,
                field_send.at[phase, 1],
                field_recv.at[phase, 1],
                lax.div(other, grp),
                lax.rem(other, grp),
            )

        wide = jnp.concatenate([field[leaves + l] for l in range(leaves)], axis=1)
        sent = nt(wide, send_basis[...]).astype(bf16)
        mine = grp + z
        coef[mine, 0] = sent[:, :LANES]
        coef[mine, 1] = sent[:, LANES:]

        for step in range(1, grp):
            send(
                coef.at[mine],
                coef.at[mine],
                coef_send.at[phase, 1],
                coef_recv.at[phase, 1],
                row,
                lax.rem(z + step, grp),
            )

        @pl.when(row > 0)
        def _():
            for other in range(grp):
                send(
                    coef.at[mine],
                    coef.at[2 * grp + z],
                    coef_send.at[phase, 0],
                    coef_recv.at[phase, 2],
                    row - 1,
                    other,
                )

        @pl.when(row < rows - 1)
        def _():
            for other in range(grp):
                send(
                    coef.at[mine],
                    coef.at[z],
                    coef_send.at[phase, 2],
                    coef_recv.at[phase, 0],
                    row + 1,
                    other,
                )

        after_send()
        before_near()
        for l in range(leaves):
            result[l] = nt(field[leaves + l], near_blocks[l, 0])

        if grp > 1:
            wait_bytes(coef.at[pl.ds(0, grp - 1)], coef_recv.at[phase, 1])
        together = coef[grp, 1].astype(f32)
        for other in range(1, grp):
            together = together + coef[grp + other, 1].astype(f32)
        group[row] = together.astype(bf16)

        def send_group(step, carry):
            send(
                group.at[row],
                group.at[row],
                group_send.at[phase],
                group_recv.at[phase],
                lax.rem(row + step, rows),
                z,
            )
            return carry

        lax.fori_loop(1, rows, send_group, 0)

        @pl.when(me > 0)
        def _():
            wait_bytes(low, field_recv.at[phase, 0])

        @pl.when(me < devices - 1)
        def _():
            wait_bytes(high, field_recv.at[phase, 1])

        first = me * leaves - leaves
        for l in range(leaves):
            total = result[l]
            for k in range(1, near_count):
                total = total + nt(field[jnp.clip(near_cols[l, k] - first, 0, 3 * leaves - 1)], near_blocks[l, k])
            result[l] = total

        @pl.when(row > 0)
        def _():
            wait_bytes(coef.at[pl.ds(0, grp)], coef_recv.at[phase, 0])

        @pl.when(row < rows - 1)
        def _():
            wait_bytes(coef.at[pl.ds(0, grp)], coef_recv.at[phase, 2])

        def slot(box):
            return jnp.clip(box - (row * grp - grp), 0, 3 * grp - 1)

        parts = []
        for l in range(leaves):
            picked = jnp.concatenate(
                [
                    coef[slot(lax.div(leaf_far[l, k], leaves)), 0]
                    for k in range(leaf_slots)
                ],
                axis=1,
            )
            parts.append(nt(picked, leaf_weights[l]))
        local = jnp.concatenate(parts, axis=1)
        picked = jnp.concatenate(
            [coef[slot(box_far[0, k]), 1] for k in range(box_slots)], axis=1
        )
        local = local + nt(picked, box_weights[...])
        if rows > 1:
            wait_bytes(group.at[pl.ds(0, rows - 1)], group_recv.at[phase])
        picked = jnp.concatenate([group[coarse_far[0, k]] for k in range(coarse_slots)], axis=1)
        local = local + nt(picked, group_weights[...])
        far = jnp.dot(local.astype(bf16), receive_basis[...], preferred_element_type=f32)
        for l in range(leaves):
            result[l] = result[l] + far[:, l * cells : (l + 1) * cells]

    def drain(phase, field, coef, group):
        own = field.at[pl.ds(leaves, leaves)]

        @pl.when(me < devices - 1)
        def _():
            wait_bytes(own, field_send.at[phase, 0])

        @pl.when(me > 0)
        def _():
            wait_bytes(own, field_send.at[phase, 1])

        @pl.when(row > 0)
        def _():
            wait_bytes(coef.at[pl.ds(0, grp)], coef_send.at[phase, 0])

        if grp > 1:
            wait_bytes(coef.at[pl.ds(0, grp - 1)], coef_send.at[phase, 1])

        @pl.when(row < rows - 1)
        def _():
            wait_bytes(coef.at[pl.ds(0, grp)], coef_send.at[phase, 2])

        if rows > 1:
            wait_bytes(group.at[pl.ds(0, rows - 1)], group_send.at[phase])

    sub_at = lax.broadcasted_iota(jnp.int32, (rhs, LANES), 0)
    lane_at = lax.broadcasted_iota(jnp.int32, (rhs, LANES), 1)

    def start_sums(index, sums, products):
        spread = jnp.zeros((rhs, LANES), f32)
        for n, product in enumerate(products):
            column = jnp.sum(product, axis=1, keepdims=True)
            spread = jnp.where(lane_at == sub_at + n * rhs, column, spread)
        sums[me] = jnp.sum(spread, axis=0, keepdims=True)

        def send_sums(step, carry):
            other = lax.rem(me + step, devices)
            send(
                sums.at[me],
                sums.at[me],
                sums_send.at[index],
                sums_recv.at[index],
                lax.div(other, grp),
                lax.rem(other, grp),
            )
            return carry

        lax.fori_loop(1, devices, send_sums, 0)

    def finish_sums(index, sums, count):
        wait_bytes(sums.at[pl.ds(0, devices - 1)], sums_recv.at[index])
        line = jnp.sum(sums[...], axis=0) / total_count
        spread = jnp.broadcast_to(line, (rhs, LANES))
        return [
            jnp.sum(jnp.where(lane_at == sub_at + n * rhs, spread, 0.0), axis=1, keepdims=True)
            for n in range(count)
        ]

    def products(pairs):
        sums = []
        for left, right in pairs:
            total = left[0] * right[0]
            for l in range(1, leaves):
                total = total + left[l] * right[l]
            sums.append(total)
        return sums

    def start_first_sums():
        start_sums(
            0, sums_a, products([(vector, vector), (vector, image), (image, image)])
        )

    operator(0, vector, image, field_a, coef_a, group_a, prepare_receive, loads[5].wait)
    operator(
        1, image, image_two, field_b, coef_b, group_b, start_first_sums, lambda: None
    )

    vv, vu, uu = finish_sums(0, sums_a, 3)
    norm_first = jnp.sqrt(vv + epsilon)
    scale_first = 1.0 / norm_first
    first_square = vv * scale_first * scale_first
    proj_first = (0.5 * vv + vu) * scale_first * scale_first
    shift = 0.5 - proj_first
    image_square = (uu + 2.0 * shift * vu + shift * shift * vv) * scale_first * scale_first
    norm_image = jnp.sqrt(jnp.maximum(image_square, 0.0) + epsilon)
    scale = scale_first / norm_image
    for l in range(leaves):
        basis = (image[l] + shift * vector[l]) * scale
        basis_out[l] = basis
        remainder_out[l] = 0.5 * basis + (image_two[l] + shift * image[l]) * scale
    start_sums(
        1,
        sums_b,
        products(
            [
                (vector, remainder_out),
                (basis_out, remainder_out),
                (remainder_out, remainder_out),
                (basis_out, vector),
                (basis_out, basis_out),
            ]
        ),
    )
    drain(0, field_a, coef_a, group_a)
    drain(1, field_b, coef_b, group_b)
    wait_bytes(sums_a.at[pl.ds(0, devices - 1)], sums_send.at[0])
    first_with, basis_with, square_two, cross_term, basis_square = finish_sums(1, sums_b, 5)
    first_with = first_with * scale_first
    cross_term = cross_term * scale_first
    proj_basis = basis_with - first_with * cross_term
    first_part = first_with * scale_first
    for l in range(leaves):
        remainder_out[l] = (
            remainder_out[l] - first_part * vector[l] - proj_basis * basis_out[l]
        )
    last_square = (
        square_two
        + first_with * first_with * first_square
        + proj_basis * proj_basis * basis_square
        - 2.0 * first_with * first_with
        - 2.0 * proj_basis * basis_with
        + 2.0 * first_with * proj_basis * cross_term
    )
    norm_last = jnp.sqrt(jnp.maximum(last_square, 0.0) + epsilon)
    for n, entry in enumerate([proj_first, norm_image, first_with, proj_basis, norm_last]):
        line = jnp.sum(jnp.where(lane_at == sub_at, entry, 0.0), axis=0, keepdims=True)
        hessenberg_out[n : n + 1, :] = line[:, :rhs]
    wait_bytes(sums_b.at[pl.ds(0, devices - 1)], sums_send.at[1])


def shards(
    rows,
    grp,
    vector,
    near_cols,
    near_blocks,
    col_basis,
    row_basis,
    leaf_far,
    leaf_coupling,
    leaf_transfer,
    box_far,
    box_coupling,
    box_transfer,
    coarse_far,
    coarse_coupling,
):
    leaves, rhs, cells = vector.shape
    rank = col_basis.shape[1]
    devices = rows * grp
    assert leaves * rank == LANES and box_far.shape[0] == 1 and coarse_far.shape[0] == 1
    assert 5 * rhs <= LANES
    vmem = pl.BlockSpec(memory_space=pltpu.VMEM)
    dma = pltpu.SemaphoreType.DMA
    operands = (
        near_cols,
        leaf_far,
        box_far,
        coarse_far,
        vector,
        near_blocks,
        col_basis,
        row_basis,
        leaf_coupling,
        leaf_transfer,
        box_coupling,
        box_transfer,
        coarse_coupling,
    )
    basis, remainder, entries = pl.pallas_call(
        functools.partial(kernel, rows, grp),
        out_shape=(
            jax.ShapeDtypeStruct(vector.shape, f32),
            jax.ShapeDtypeStruct(vector.shape, f32),
            jax.ShapeDtypeStruct((5, rhs), f32),
        ),
        in_specs=[pl.BlockSpec(memory_space=pltpu.HBM)] * len(operands),
        out_specs=(vmem, vmem, vmem),
        scratch_shapes=[
            *[pltpu.SMEM(operand.shape, operand.dtype) for operand in operands[:4]],
            *[pltpu.VMEM(operand.shape, operand.dtype) for operand in operands[4:]],
            pltpu.VMEM((3 * leaves, rhs, cells), bf16),
            pltpu.VMEM((3 * leaves, rhs, cells), bf16),
            pltpu.VMEM((3 * grp, 2, rhs, LANES), bf16),
            pltpu.VMEM((3 * grp, 2, rhs, LANES), bf16),
            pltpu.VMEM((rows, rhs, LANES), bf16),
            pltpu.VMEM((rows, rhs, LANES), bf16),
            pltpu.VMEM((devices, 1, LANES), f32),
            pltpu.VMEM((devices, 1, LANES), f32),
            pltpu.VMEM((2 * LANES, leaves * cells), bf16),
            pltpu.VMEM((LANES, leaves * cells), bf16),
            pltpu.VMEM((leaves, rank, leaf_far.shape[1] * LANES), bf16),
            pltpu.VMEM((LANES, box_far.shape[1] * LANES), bf16),
            pltpu.VMEM((LANES, coarse_far.shape[1] * LANES), bf16),
            pltpu.VMEM(vector.shape, f32),
            pltpu.VMEM(vector.shape, f32),
            dma((len(operands),)),
            dma((2, 2)),
            dma((2, 2)),
            dma((2, 3)),
            dma((2, 3)),
            dma((2,)),
            dma((2,)),
            dma((2,)),
            dma((2,)),
        ],
        compiler_params=pltpu.CompilerParams(
            collective_id=0, has_side_effects=True, vmem_limit_bytes=65100 * 1024
        ),
    )(*operands)
    return basis, remainder, entries.T


def solution(mesh):
    return jax.shard_map(
        functools.partial(shards, mesh.shape["rows"], mesh.shape["grp"]),
        mesh=mesh,
        in_specs=(
            P(("rows", "grp"), None, None),
            P(("rows", "grp"), None),
            P(("rows", "grp"), None, None, None),
            P(("rows", "grp"), None, None),
            P(("rows", "grp"), None, None),
            P(("rows", "grp"), None),
            P(("rows", "grp"), None, None),
            P(("rows", "grp"), None, None),
            P(("rows", "grp"), None),
            P(("rows", "grp"), None, None),
            P(("rows", "grp"), None, None),
            P("rows", None),
            P("rows", None, None),
        ),
        out_specs=(P(("rows", "grp"), None, None), P(("rows", "grp"), None, None), P()),
        check_vma=False,
    )
```

```python
import functools

import jax
import jax.numpy as jnp
from jax import lax
from jax.experimental import pallas as pl
from jax.experimental.pallas import tpu as pltpu
from jax.sharding import PartitionSpec as P

LANES = 128
epsilon = 1e-06
highest = lax.Precision.HIGHEST
MESH = pl.DeviceIdType.MESH
bf16 = jnp.bfloat16
f32 = jnp.float32


def nt(left, right, precision=None):
    return lax.dot_general(
        left, right, (((1,), (1,)), ((), ())), precision=precision, preferred_element_type=f32
    )


def wrap(index, size):
    return jnp.where(index >= size, index - size, index)


def kernel(
    rows,
    grp,
    *refs,
):
    sources = refs[:13]
    results = refs[13:16]
    targets = refs[16:29]
    (
        near_cols,
        leaf_far,
        box_far,
        coarse_far,
        vector,
        near_blocks,
        col_basis,
        row_basis,
        leaf_coupling,
        leaf_transfer,
        box_coupling,
        box_transfer,
        coarse_coupling,
    ) = targets
    (
        field_a,
        field_b,
        coef_a,
        coef_b,
        group_a,
        group_b,
        sums_a,
        sums_b,
        send_basis,
        receive_basis,
        leaf_weights,
        box_weights,
        group_weights,
        image,
        image_two,
        select,
        basis_out,
        remainder_out,
        hessenberg_out,
        store_sem,
        load_sem,
        field_send,
        field_recv,
        coef_send,
        coef_recv,
        group_send,
        group_recv,
        sums_send,
        sums_recv,
    ) = refs[29:]
    leaves, rhs, cells = vector.shape
    rank = col_basis.shape[1]
    near_count = near_cols.shape[1]
    leaf_slots = leaf_far.shape[1]
    box_slots = box_far.shape[1]
    coarse_slots = coarse_far.shape[1]
    devices = rows * grp
    total_count = leaves * devices * cells
    row = lax.axis_index("rows")
    z = lax.axis_index("grp")
    me = row * grp + z

    loads = [
        pltpu.make_async_copy(source, target, load_sem.at[n])
        for n, (source, target) in enumerate(zip(sources, targets))
    ]
    for n in (4, 6, 9, 11, 7, 8, 10, 12, 0, 1, 2, 3, 5):
        loads[n].start()

    barrier = pltpu.get_barrier_semaphore()

    def each_other(visit):
        def one_row(step, carry):
            to_row = wrap(row + step, rows)
            for turn in range(grp):
                visit(to_row, wrap(z + turn, grp))
            return carry

        for turn in range(1, grp):
            visit(row, wrap(z + turn, grp))
        lax.fori_loop(1, rows, one_row, 0)

    def greet(to_row, to_z):
        pl.semaphore_signal(barrier, inc=1, device_id=(to_row, to_z), device_id_type=MESH)

    each_other(greet)

    send_basis[...] = jnp.zeros_like(send_basis)
    for n in (4, 6, 9, 11):
        loads[n].wait()
    for l in range(leaves):
        send_basis[l * rank : (l + 1) * rank, l * cells : (l + 1) * cells] = col_basis[l]
    width = leaves * rank
    transfer = leaf_transfer[...].reshape(width, rank)
    down = jnp.dot(transfer, box_transfer[0], precision=highest, preferred_element_type=f32)
    up = jnp.concatenate([transfer, down], axis=1).T
    up_high = up.astype(bf16)
    up_low = (up - up_high.astype(f32)).astype(bf16)
    plain = send_basis[:width]
    send_basis[width : width + 2 * rank] = (
        jnp.dot(up_high, plain, preferred_element_type=f32)
        + jnp.dot(up_low, plain, preferred_element_type=f32)
    ).astype(bf16)

    def prepare_receive():
        for n in (7, 8, 10, 12, 0, 1, 2, 3):
            loads[n].wait()
        receive_basis[...] = jnp.zeros_like(receive_basis)
        for l in range(leaves):
            receive_basis[l * rank : (l + 1) * rank, l * cells : (l + 1) * cells] = row_basis[l]
        lane = lax.broadcasted_iota(jnp.int32, (rank, LANES), 1)
        unit = lax.broadcasted_iota(jnp.int32, (rank, LANES), 0)
        select[...] = jnp.zeros_like(select)
        for k in range(select.shape[0] // rank):
            select[k * rank : (k + 1) * rank, k * LANES : (k + 1) * LANES] = jnp.where(
                (lane & (rank - 1)) == unit, 1.0, 0.0
            ).astype(bf16)
        tiled = jnp.dot(
            leaf_coupling[...].reshape(width, leaf_slots * rank),
            select[: leaf_slots * rank, : leaf_slots * LANES],
            preferred_element_type=f32,
        )
        for l in range(leaves):
            for k in range(leaf_slots):
                start = lax.rem(leaf_far[l, k], leaves) * rank
                piece = tiled[l * rank : (l + 1) * rank, k * LANES : (k + 1) * LANES]
                leaf_weights[l, :, k * LANES : (k + 1) * LANES] = jnp.where(
                    (lane >= start) & (lane < start + rank), piece, 0.0
                ).astype(bf16)

        def compose(target, coupling, above, low):
            slots = coupling.shape[1] // rank
            wide = jnp.dot(
                coupling, select[: slots * rank, : slots * LANES], preferred_element_type=f32
            )
            place = lax.broadcasted_iota(jnp.int32, wide.shape, 1) & (LANES - 1)
            wide = jnp.where((place >= low) & (place < low + rank), wide, 0.0).astype(bf16)
            above_high = above.astype(bf16)
            above_low = (above - above_high.astype(f32)).astype(bf16)
            target[...] = (
                jnp.dot(above_high, wide, preferred_element_type=f32)
                + jnp.dot(above_low, wide, preferred_element_type=f32)
            ).astype(bf16)

        compose(box_weights, box_coupling[0], transfer, 0)
        compose(group_weights, coarse_coupling[0], down, rank)

    def send(src, dst, send_sem, recv_sem, to_row, to_z):
        pltpu.make_async_remote_copy(
            src_ref=src,
            dst_ref=dst,
            send_sem=send_sem,
            recv_sem=recv_sem,
            device_id=(to_row, to_z),
            device_id_type=MESH,
        ).start()

    def wait_bytes(ref, sem):
        pltpu.make_async_copy(ref, ref, sem).wait()

    def operator(phase, source, result, field, coef, group, after_send, before_near):
        for l in range(leaves):
            field[leaves + l] = source[l].astype(bf16)
        if phase == 0:
            pl.semaphore_wait(barrier, devices - 1)
        own = field.at[pl.ds(leaves, leaves)]
        low = field.at[pl.ds(0, leaves)]
        high = field.at[pl.ds(2 * leaves, leaves)]

        @pl.when(me < devices - 1)
        def _():
            last = z == grp - 1
            send(
                own,
                low,
                field_send.at[phase, 0],
                field_recv.at[phase, 0],
                jnp.where(last, row + 1, row),
                jnp.where(last, 0, z + 1),
            )

        @pl.when(me > 0)
        def _():
            send(
                own,
                high,
                field_send.at[phase, 1],
                field_recv.at[phase, 1],
                jnp.where(z == 0, row - 1, row),
                jnp.where(z == 0, grp - 1, z - 1),
            )

        wide = jnp.concatenate([field[leaves + l] for l in range(leaves)], axis=1)
        sent = nt(wide, send_basis[...]).astype(bf16)
        mine = grp + z
        coef[mine, 0] = sent[:, :LANES]
        coef[mine, 1] = sent[:, LANES:]

        for step in range(1, grp):
            send(
                coef.at[mine],
                coef.at[mine],
                coef_send.at[phase, 1],
                coef_recv.at[phase, 1],
                row,
                wrap(z + step, grp),
            )

        @pl.when(row > 0)
        def _():
            for other in range(grp):
                send(
                    coef.at[mine],
                    coef.at[2 * grp + z],
                    coef_send.at[phase, 0],
                    coef_recv.at[phase, 2],
                    row - 1,
                    other,
                )

        @pl.when(row < rows - 1)
        def _():
            for other in range(grp):
                send(
                    coef.at[mine],
                    coef.at[z],
                    coef_send.at[phase, 2],
                    coef_recv.at[phase, 0],
                    row + 1,
                    other,
                )

        after_send()
        before_near()
        for l in range(leaves):
            result[l] = nt(field[leaves + l], near_blocks[l, 0])

        if grp > 1:
            wait_bytes(coef.at[pl.ds(0, grp - 1)], coef_recv.at[phase, 1])
        together = coef[grp, 1].astype(f32)
        for other in range(1, grp):
            together = together + coef[grp + other, 1].astype(f32)
        group[row] = together.astype(bf16)

        def send_group(step, carry):
            send(
                group.at[row],
                group.at[row],
                group_send.at[phase],
                group_recv.at[phase],
                wrap(row + step, rows),
                z,
            )
            return carry

        lax.fori_loop(1, rows, send_group, 0)

        @pl.when(me > 0)
        def _():
            wait_bytes(low, field_recv.at[phase, 0])

        @pl.when(me < devices - 1)
        def _():
            wait_bytes(high, field_recv.at[phase, 1])

        first = me * leaves - leaves
        for l in range(leaves):
            total = result[l]
            for k in range(1, near_count):
                total = total + nt(field[jnp.clip(near_cols[l, k] - first, 0, 3 * leaves - 1)], near_blocks[l, k])
            result[l] = total

        @pl.when(row > 0)
        def _():
            wait_bytes(coef.at[pl.ds(0, grp)], coef_recv.at[phase, 0])

        @pl.when(row < rows - 1)
        def _():
            wait_bytes(coef.at[pl.ds(0, grp)], coef_recv.at[phase, 2])

        def slot(box):
            return jnp.clip(box - (row * grp - grp), 0, 3 * grp - 1)

        parts = []
        for l in range(leaves):
            picked = jnp.concatenate(
                [
                    coef[slot(lax.div(leaf_far[l, k], leaves)), 0]
                    for k in range(leaf_slots)
                ],
                axis=1,
            )
            parts.append(nt(picked, leaf_weights[l]))
        local = jnp.concatenate(parts, axis=1)
        picked = jnp.concatenate(
            [coef[slot(box_far[0, k]), 1] for k in range(box_slots)], axis=1
        )
        local = local + nt(picked, box_weights[...])
        if rows > 1:
            wait_bytes(group.at[pl.ds(0, rows - 1)], group_recv.at[phase])
        picked = jnp.concatenate([group[coarse_far[0, k]] for k in range(coarse_slots)], axis=1)
        local = local + nt(picked, group_weights[...])
        far = jnp.dot(local.astype(bf16), receive_basis[...], preferred_element_type=f32)
        for l in range(leaves):
            result[l] = result[l] + far[:, l * cells : (l + 1) * cells]

    def drain(phase, field, coef, group):
        own = field.at[pl.ds(leaves, leaves)]

        @pl.when(me < devices - 1)
        def _():
            wait_bytes(own, field_send.at[phase, 0])

        @pl.when(me > 0)
        def _():
            wait_bytes(own, field_send.at[phase, 1])

        @pl.when(row > 0)
        def _():
            wait_bytes(coef.at[pl.ds(0, grp)], coef_send.at[phase, 0])

        if grp > 1:
            wait_bytes(coef.at[pl.ds(0, grp - 1)], coef_send.at[phase, 1])

        @pl.when(row < rows - 1)
        def _():
            wait_bytes(coef.at[pl.ds(0, grp)], coef_send.at[phase, 2])

        if rows > 1:
            wait_bytes(group.at[pl.ds(0, rows - 1)], group_send.at[phase])

    sub_at = lax.broadcasted_iota(jnp.int32, (rhs, LANES), 0)
    lane_at = lax.broadcasted_iota(jnp.int32, (rhs, LANES), 1)

    def start_sums(index, sums, products):
        spread = jnp.zeros((rhs, LANES), f32)
        for n, product in enumerate(products):
            column = jnp.sum(product, axis=1, keepdims=True)
            spread = jnp.where(lane_at == sub_at + n * rhs, column, spread)
        sums[me] = jnp.sum(spread, axis=0, keepdims=True)

        def send_sums(to_row, to_z):
            send(
                sums.at[me],
                sums.at[me],
                sums_send.at[index],
                sums_recv.at[index],
                to_row,
                to_z,
            )

        each_other(send_sums)

    def finish_sums(index, sums, count):
        wait_bytes(sums.at[pl.ds(0, devices - 1)], sums_recv.at[index])
        line = jnp.sum(sums[...], axis=0) / total_count
        spread = jnp.broadcast_to(line, (rhs, LANES))
        return [
            jnp.sum(jnp.where(lane_at == sub_at + n * rhs, spread, 0.0), axis=1, keepdims=True)
            for n in range(count)
        ]

    def products(pairs):
        sums = []
        for left, right in pairs:
            total = left[0] * right[0]
            for l in range(1, leaves):
                total = total + left[l] * right[l]
            sums.append(total)
        return sums

    def start_first_sums():
        start_sums(
            0, sums_a, products([(vector, vector), (vector, image), (image, image)])
        )

    operator(0, vector, image, field_a, coef_a, group_a, prepare_receive, loads[5].wait)
    operator(
        1, image, image_two, field_b, coef_b, group_b, start_first_sums, lambda: None
    )

    vv, vu, uu = finish_sums(0, sums_a, 3)
    norm_first = jnp.sqrt(vv + epsilon)
    scale_first = 1.0 / norm_first
    first_square = vv * scale_first * scale_first
    proj_first = (0.5 * vv + vu) * scale_first * scale_first
    shift = 0.5 - proj_first
    image_square = (uu + 2.0 * shift * vu + shift * shift * vv) * scale_first * scale_first
    norm_image = jnp.sqrt(jnp.maximum(image_square, 0.0) + epsilon)
    scale = scale_first / norm_image
    stores = [
        pltpu.make_async_copy(source, result, store_sem.at[n])
        for n, (source, result) in enumerate(
            zip((basis_out, remainder_out, hessenberg_out), results)
        )
    ]
    for l in range(leaves):
        basis = (image[l] + shift * vector[l]) * scale
        basis_out[l] = basis
        remainder_out[l] = 0.5 * basis + (image_two[l] + shift * image[l]) * scale
    start_sums(
        1,
        sums_b,
        products(
            [
                (vector, remainder_out),
                (basis_out, remainder_out),
                (remainder_out, remainder_out),
                (basis_out, vector),
                (basis_out, basis_out),
            ]
        ),
    )
    stores[0].start()
    drain(0, field_a, coef_a, group_a)
    drain(1, field_b, coef_b, group_b)
    wait_bytes(sums_a.at[pl.ds(0, devices - 1)], sums_send.at[0])
    first_with, basis_with, square_two, cross_term, basis_square = finish_sums(1, sums_b, 5)
    first_with = first_with * scale_first
    cross_term = cross_term * scale_first
    proj_basis = basis_with - first_with * cross_term
    first_part = first_with * scale_first
    for l in range(leaves):
        remainder_out[l] = (
            remainder_out[l] - first_part * vector[l] - proj_basis * basis_out[l]
        )
    stores[1].start()
    last_square = (
        square_two
        + first_with * first_with * first_square
        + proj_basis * proj_basis * basis_square
        - 2.0 * first_with * first_with
        - 2.0 * proj_basis * basis_with
        + 2.0 * first_with * proj_basis * cross_term
    )
    norm_last = jnp.sqrt(jnp.maximum(last_square, 0.0) + epsilon)
    for n, entry in enumerate([proj_first, norm_image, first_with, proj_basis, norm_last]):
        line = jnp.sum(jnp.where(lane_at == sub_at, entry, 0.0), axis=0, keepdims=True)
        hessenberg_out[n : n + 1, :] = line[:, :rhs]
    stores[2].start()
    wait_bytes(sums_b.at[pl.ds(0, devices - 1)], sums_send.at[1])
    for store in stores:
        store.wait()


def hand_on(*refs):
    copies = [
        pltpu.make_async_copy(refs[n], refs[3 + n], refs[6].at[n]) for n in range(3)
    ]
    for copy in copies:
        copy.start()
    for copy in copies:
        copy.wait()


def shards(
    rows,
    grp,
    vector,
    near_cols,
    near_blocks,
    col_basis,
    row_basis,
    leaf_far,
    leaf_coupling,
    leaf_transfer,
    box_far,
    box_coupling,
    box_transfer,
    coarse_far,
    coarse_coupling,
):
    leaves, rhs, cells = vector.shape
    rank = col_basis.shape[1]
    devices = rows * grp
    assert leaves * rank == LANES and box_far.shape[0] == 1 and coarse_far.shape[0] == 1
    assert 5 * rhs <= LANES and rank & (rank - 1) == 0
    hbm = pl.BlockSpec(memory_space=pltpu.HBM)
    slots = max(leaf_far.shape[1], box_far.shape[1], coarse_far.shape[1])
    dma = pltpu.SemaphoreType.DMA
    operands = (
        near_cols,
        leaf_far,
        box_far,
        coarse_far,
        vector,
        near_blocks,
        col_basis,
        row_basis,
        leaf_coupling,
        leaf_transfer,
        box_coupling,
        box_transfer,
        coarse_coupling,
    )
    shapes = (
        jax.ShapeDtypeStruct(vector.shape, f32),
        jax.ShapeDtypeStruct(vector.shape, f32),
        jax.ShapeDtypeStruct((5, rhs), f32),
    )
    results = pl.pallas_call(
        functools.partial(kernel, rows, grp),
        out_shape=shapes,
        in_specs=[hbm] * len(operands),
        out_specs=(hbm, hbm, hbm),
        scratch_shapes=[
            *[pltpu.SMEM(operand.shape, operand.dtype) for operand in operands[:4]],
            *[pltpu.VMEM(operand.shape, operand.dtype) for operand in operands[4:]],
            pltpu.VMEM((3 * leaves, rhs, cells), bf16),
            pltpu.VMEM((3 * leaves, rhs, cells), bf16),
            pltpu.VMEM((3 * grp, 2, rhs, LANES), bf16),
            pltpu.VMEM((3 * grp, 2, rhs, LANES), bf16),
            pltpu.VMEM((rows, rhs, LANES), bf16),
            pltpu.VMEM((rows, rhs, LANES), bf16),
            pltpu.VMEM((devices, 1, LANES), f32),
            pltpu.VMEM((devices, 1, LANES), f32),
            pltpu.VMEM((2 * LANES, leaves * cells), bf16),
            pltpu.VMEM((LANES, leaves * cells), bf16),
            pltpu.VMEM((leaves, rank, leaf_far.shape[1] * LANES), bf16),
            pltpu.VMEM((LANES, box_far.shape[1] * LANES), bf16),
            pltpu.VMEM((LANES, coarse_far.shape[1] * LANES), bf16),
            pltpu.VMEM(vector.shape, f32),
            pltpu.VMEM(vector.shape, f32),
            pltpu.VMEM((slots * rank, slots * LANES), bf16),
            pltpu.VMEM(vector.shape, f32),
            pltpu.VMEM(vector.shape, f32),
            pltpu.VMEM((5, rhs), f32),
            dma((3,)),
            dma((len(operands),)),
            dma((2, 2)),
            dma((2, 2)),
            dma((2, 3)),
            dma((2, 3)),
            dma((2,)),
            dma((2,)),
            dma((2,)),
            dma((2,)),
        ],
        compiler_params=pltpu.CompilerParams(
            collective_id=0, has_side_effects=True, vmem_limit_bytes=65100 * 1024
        ),
    )(*operands)
    basis, remainder, entries = pl.pallas_call(
        hand_on,
        out_shape=shapes,
        in_specs=[hbm] * 3,
        out_specs=(hbm, hbm, hbm),
        scratch_shapes=[dma((3,))],
        compiler_params=pltpu.CompilerParams(vmem_limit_bytes=65100 * 1024),
    )(*results)
    return basis, remainder, entries.T


def solution(mesh):
    return jax.shard_map(
        functools.partial(shards, mesh.shape["rows"], mesh.shape["grp"]),
        mesh=mesh,
        in_specs=(
            P(("rows", "grp"), None, None),
            P(("rows", "grp"), None),
            P(("rows", "grp"), None, None, None),
            P(("rows", "grp"), None, None),
            P(("rows", "grp"), None, None),
            P(("rows", "grp"), None),
            P(("rows", "grp"), None, None),
            P(("rows", "grp"), None, None),
            P(("rows", "grp"), None),
            P(("rows", "grp"), None, None),
            P(("rows", "grp"), None, None),
            P("rows", None),
            P("rows", None, None),
        ),
        out_specs=(P(("rows", "grp"), None, None), P(("rows", "grp"), None, None), P()),
        check_vma=False,
    )
```

```python
import functools

import jax
import jax.numpy as jnp
from jax import lax
from jax.experimental import pallas as pl
from jax.experimental.pallas import tpu as pltpu
from jax.sharding import PartitionSpec as P

LANES = 128
epsilon = 1e-06
highest = lax.Precision.HIGHEST
MESH = pl.DeviceIdType.MESH
bf16 = jnp.bfloat16
f32 = jnp.float32


def nt(left, right, precision=None):
    return lax.dot_general(
        left, right, (((1,), (1,)), ((), ())), precision=precision, preferred_element_type=f32
    )


def wrap(index, size):
    return jnp.where(index >= size, index - size, index)


def kernel(
    rows,
    grp,
    *refs,
):
    sources = refs[:13]
    results = refs[13:16]
    targets = refs[16:29]
    (
        near_cols,
        leaf_far,
        box_far,
        coarse_far,
        vector,
        near_blocks,
        col_basis,
        row_basis,
        leaf_coupling,
        leaf_transfer,
        box_coupling,
        box_transfer,
        coarse_coupling,
    ) = targets
    (
        field_a,
        field_b,
        coef_a,
        coef_b,
        group_a,
        group_b,
        sums_a,
        sums_b,
        send_basis,
        receive_basis,
        leaf_weights,
        box_weights,
        group_weights,
        image,
        image_two,
        select,
        basis_out,
        remainder_out,
        hessenberg_out,
        store_sem,
        load_sem,
        field_send,
        field_recv,
        coef_send,
        coef_recv,
        group_send,
        group_recv,
        sums_send,
        sums_recv,
    ) = refs[29:]
    leaves, rhs, cells = vector.shape
    rank = col_basis.shape[1]
    near_count = near_cols.shape[1]
    leaf_slots = leaf_far.shape[1]
    box_slots = box_far.shape[1]
    coarse_slots = coarse_far.shape[1]
    devices = rows * grp
    total_count = leaves * devices * cells
    row = lax.axis_index("rows")
    z = lax.axis_index("grp")
    me = row * grp + z

    loads = [
        pltpu.make_async_copy(source, target, load_sem.at[n])
        for n, (source, target) in enumerate(zip(sources, targets))
    ]
    for n in (4, 6, 9, 11, 7, 8, 10, 12, 0, 1, 2, 3, 5):
        loads[n].start()

    barrier = pltpu.get_barrier_semaphore()

    def greet(to_row, to_z):
        pl.semaphore_signal(barrier, inc=1, device_id=(to_row, to_z), device_id_type=MESH)

    def greet_row(step, carry):
        greet(wrap(row + step, rows), z)
        return carry

    for turn in range(1, grp):
        other = wrap(z + turn, grp)
        greet(row, other)

        @pl.when(row > 0)
        def _():
            greet(row - 1, other)

        @pl.when(row < rows - 1)
        def _():
            greet(row + 1, other)

    lax.fori_loop(1, rows, greet_row, 0)
    beside = jnp.where(row > 0, 1, 0) + jnp.where(row < rows - 1, 1, 0)
    greetings = (grp - 1) * (1 + beside) + rows - 1

    send_basis[...] = jnp.zeros_like(send_basis)
    for n in (4, 6, 9, 11):
        loads[n].wait()
    for l in range(leaves):
        send_basis[l * rank : (l + 1) * rank, l * cells : (l + 1) * cells] = col_basis[l]
    width = leaves * rank
    transfer = leaf_transfer[...].reshape(width, rank)
    down = jnp.dot(transfer, box_transfer[0], precision=highest, preferred_element_type=f32)
    up = jnp.concatenate([transfer, down], axis=1).T
    up_high = up.astype(bf16)
    up_low = (up - up_high.astype(f32)).astype(bf16)
    plain = send_basis[:width]
    send_basis[width : width + 2 * rank] = (
        jnp.dot(up_high, plain, preferred_element_type=f32)
        + jnp.dot(up_low, plain, preferred_element_type=f32)
    ).astype(bf16)

    def prepare_receive():
        for n in (7, 8, 10, 12, 0, 1, 2, 3):
            loads[n].wait()
        receive_basis[...] = jnp.zeros_like(receive_basis)
        for l in range(leaves):
            receive_basis[l * rank : (l + 1) * rank, l * cells : (l + 1) * cells] = row_basis[l]
        lane = lax.broadcasted_iota(jnp.int32, (rank, LANES), 1)
        unit = lax.broadcasted_iota(jnp.int32, (rank, LANES), 0)
        select[...] = jnp.zeros_like(select)
        for k in range(select.shape[0] // rank):
            select[k * rank : (k + 1) * rank, k * LANES : (k + 1) * LANES] = jnp.where(
                (lane & (rank - 1)) == unit, 1.0, 0.0
            ).astype(bf16)
        tiled = jnp.dot(
            leaf_coupling[...].reshape(width, leaf_slots * rank),
            select[: leaf_slots * rank, : leaf_slots * LANES],
            preferred_element_type=f32,
        )
        for l in range(leaves):
            for k in range(leaf_slots):
                start = lax.rem(leaf_far[l, k], leaves) * rank
                piece = tiled[l * rank : (l + 1) * rank, k * LANES : (k + 1) * LANES]
                leaf_weights[l, :, k * LANES : (k + 1) * LANES] = jnp.where(
                    (lane >= start) & (lane < start + rank), piece, 0.0
                ).astype(bf16)

        def compose(target, coupling, above, low):
            slots = coupling.shape[1] // rank
            wide = jnp.dot(
                coupling, select[: slots * rank, : slots * LANES], preferred_element_type=f32
            )
            place = lax.broadcasted_iota(jnp.int32, wide.shape, 1) & (LANES - 1)
            wide = jnp.where((place >= low) & (place < low + rank), wide, 0.0).astype(bf16)
            above_high = above.astype(bf16)
            above_low = (above - above_high.astype(f32)).astype(bf16)
            target[...] = (
                jnp.dot(above_high, wide, preferred_element_type=f32)
                + jnp.dot(above_low, wide, preferred_element_type=f32)
            ).astype(bf16)

        compose(box_weights, box_coupling[0], transfer, 0)
        compose(group_weights, coarse_coupling[0], down, rank)

    def send(src, dst, send_sem, recv_sem, to_row, to_z):
        pltpu.make_async_remote_copy(
            src_ref=src,
            dst_ref=dst,
            send_sem=send_sem,
            recv_sem=recv_sem,
            device_id=(to_row, to_z),
            device_id_type=MESH,
        ).start()

    def wait_bytes(ref, sem):
        pltpu.make_async_copy(ref, ref, sem).wait()

    sub_at = lax.broadcasted_iota(jnp.int32, (rhs, LANES), 0)
    lane_at = lax.broadcasted_iota(jnp.int32, (rhs, LANES), 1)

    def with_sums(tile, columns):
        for n, column in enumerate(columns):
            for part in range(3):
                piece = column.astype(bf16).astype(f32)
                tile = jnp.where(lane_at == 2 * rank + 3 * n + part, piece, tile)
                column = column - piece
        return tile

    def read_sums(tile, count):
        return [
            jnp.sum(
                jnp.where(
                    (lane_at >= 2 * rank + 3 * n) & (lane_at < 2 * rank + 3 * n + 3), tile, 0.0
                ),
                axis=1,
                keepdims=True,
            )
            for n in range(count)
        ]

    def operator(phase, source, result, field, coef, group, sums, after_send, before_near):
        for l in range(leaves):
            field[leaves + l] = source[l].astype(bf16)
        if phase == 0:
            pl.semaphore_wait(barrier, greetings)
        own = field.at[pl.ds(leaves, leaves)]
        low = field.at[pl.ds(0, leaves)]
        high = field.at[pl.ds(2 * leaves, leaves)]

        @pl.when(me < devices - 1)
        def _():
            last = z == grp - 1
            send(
                own,
                low,
                field_send.at[phase, 0],
                field_recv.at[phase, 0],
                jnp.where(last, row + 1, row),
                jnp.where(last, 0, z + 1),
            )

        @pl.when(me > 0)
        def _():
            send(
                own,
                high,
                field_send.at[phase, 1],
                field_recv.at[phase, 1],
                jnp.where(z == 0, row - 1, row),
                jnp.where(z == 0, grp - 1, z - 1),
            )

        wide = jnp.concatenate([field[leaves + l] for l in range(leaves)], axis=1)
        sent = nt(wide, send_basis[...])
        mine = grp + z
        coef[mine, 0] = sent[:, :LANES].astype(bf16)
        coef[mine, 1] = with_sums(sent[:, LANES:], sums()).astype(bf16)

        for step in range(1, grp):
            send(
                coef.at[mine],
                coef.at[mine],
                coef_send.at[phase, 1],
                coef_recv.at[phase, 1],
                row,
                wrap(z + step, grp),
            )

        @pl.when(row > 0)
        def _():
            for other in range(grp):
                send(
                    coef.at[mine],
                    coef.at[2 * grp + z],
                    coef_send.at[phase, 0],
                    coef_recv.at[phase, 2],
                    row - 1,
                    other,
                )

        @pl.when(row < rows - 1)
        def _():
            for other in range(grp):
                send(
                    coef.at[mine],
                    coef.at[z],
                    coef_send.at[phase, 2],
                    coef_recv.at[phase, 0],
                    row + 1,
                    other,
                )

        after_send()
        before_near()
        for l in range(leaves):
            result[l] = nt(field[leaves + l], near_blocks[l, 0])

        if grp > 1:
            wait_bytes(coef.at[pl.ds(0, grp - 1)], coef_recv.at[phase, 1])
        together = coef[grp, 1].astype(f32)
        for other in range(1, grp):
            together = together + coef[grp + other, 1].astype(f32)
        if phase == 1:
            together = with_sums(together, read_sums(together, 3))
        group[row] = together.astype(bf16)

        def send_group(step, carry):
            send(
                group.at[row],
                group.at[row],
                group_send.at[phase],
                group_recv.at[phase],
                wrap(row + step, rows),
                z,
            )
            return carry

        lax.fori_loop(1, rows, send_group, 0)

        @pl.when(me > 0)
        def _():
            wait_bytes(low, field_recv.at[phase, 0])

        @pl.when(me < devices - 1)
        def _():
            wait_bytes(high, field_recv.at[phase, 1])

        first = me * leaves - leaves
        for l in range(leaves):
            total = result[l]
            for k in range(1, near_count):
                total = total + nt(field[jnp.clip(near_cols[l, k] - first, 0, 3 * leaves - 1)], near_blocks[l, k])
            result[l] = total

        @pl.when(row > 0)
        def _():
            wait_bytes(coef.at[pl.ds(0, grp)], coef_recv.at[phase, 0])

        @pl.when(row < rows - 1)
        def _():
            wait_bytes(coef.at[pl.ds(0, grp)], coef_recv.at[phase, 2])

        def slot(box):
            return jnp.clip(box - (row * grp - grp), 0, 3 * grp - 1)

        parts = []
        for l in range(leaves):
            picked = jnp.concatenate(
                [
                    coef[slot(lax.div(leaf_far[l, k], leaves)), 0]
                    for k in range(leaf_slots)
                ],
                axis=1,
            )
            parts.append(nt(picked, leaf_weights[l]))
        local = jnp.concatenate(parts, axis=1)
        picked = jnp.concatenate(
            [coef[slot(box_far[0, k]), 1] for k in range(box_slots)], axis=1
        )
        local = local + nt(picked, box_weights[...])
        if rows > 1:
            wait_bytes(group.at[pl.ds(0, rows - 1)], group_recv.at[phase])
        picked = jnp.concatenate([group[coarse_far[0, k]] for k in range(coarse_slots)], axis=1)
        local = local + nt(picked, group_weights[...])
        far = jnp.dot(local.astype(bf16), receive_basis[...], preferred_element_type=f32)
        for l in range(leaves):
            result[l] = result[l] + far[:, l * cells : (l + 1) * cells]

    def drain(phase, field, coef, group):
        own = field.at[pl.ds(leaves, leaves)]

        @pl.when(me < devices - 1)
        def _():
            wait_bytes(own, field_send.at[phase, 0])

        @pl.when(me > 0)
        def _():
            wait_bytes(own, field_send.at[phase, 1])

        @pl.when(row > 0)
        def _():
            wait_bytes(coef.at[pl.ds(0, grp)], coef_send.at[phase, 0])

        if grp > 1:
            wait_bytes(coef.at[pl.ds(0, grp - 1)], coef_send.at[phase, 1])

        @pl.when(row < rows - 1)
        def _():
            wait_bytes(coef.at[pl.ds(0, grp)], coef_send.at[phase, 2])

        if rows > 1:
            wait_bytes(group.at[pl.ds(0, rows - 1)], group_send.at[phase])

    def start_sums(columns):
        spread = jnp.zeros((rhs, LANES), f32)
        for n, column in enumerate(columns):
            spread = jnp.where(lane_at == sub_at + n * rhs, column, spread)
        sums_a[z] = jnp.sum(spread, axis=0, keepdims=True)
        for turn in range(1, grp):
            send(
                sums_a.at[z],
                sums_a.at[z],
                sums_send.at[0],
                sums_recv.at[0],
                row,
                wrap(z + turn, grp),
            )

    def finish_sums(count):
        if grp > 1:
            wait_bytes(sums_a.at[pl.ds(0, grp - 1)], sums_recv.at[0])
        sums_b[row] = jnp.sum(sums_a[...], axis=0)

        def send_sums(step, carry):
            send(
                sums_b.at[row],
                sums_b.at[row],
                sums_send.at[1],
                sums_recv.at[1],
                wrap(row + step, rows),
                z,
            )
            return carry

        lax.fori_loop(1, rows, send_sums, 0)
        if rows > 1:
            wait_bytes(sums_b.at[pl.ds(0, rows - 1)], sums_recv.at[1])
        line = jnp.sum(sums_b[...], axis=0) / total_count
        spread = jnp.broadcast_to(line, (rhs, LANES))
        return [
            jnp.sum(jnp.where(lane_at == sub_at + n * rhs, spread, 0.0), axis=1, keepdims=True)
            for n in range(count)
        ]

    def products(pairs):
        sums = []
        for left, right in pairs:
            total = left[0] * right[0]
            for l in range(1, leaves):
                total = total + left[l] * right[l]
            sums.append(jnp.sum(total, axis=1, keepdims=True))
        return sums

    def first_sums():
        return products([(vector, vector), (vector, image), (image, image)])

    operator(
        0,
        vector,
        image,
        field_a,
        coef_a,
        group_a,
        lambda: [],
        prepare_receive,
        loads[5].wait,
    )
    operator(
        1,
        image,
        image_two,
        field_b,
        coef_b,
        group_b,
        first_sums,
        lambda: None,
        lambda: None,
    )

    together = group_b[0].astype(f32)
    for n in range(1, rows):
        together = together + group_b[n].astype(f32)
    vv, vu, uu = [column / total_count for column in read_sums(together, 3)]
    norm_first = jnp.sqrt(vv + epsilon)
    scale_first = 1.0 / norm_first
    first_square = vv * scale_first * scale_first
    proj_first = (0.5 * vv + vu) * scale_first * scale_first
    shift = 0.5 - proj_first
    image_square = (uu + 2.0 * shift * vu + shift * shift * vv) * scale_first * scale_first
    norm_image = jnp.sqrt(jnp.maximum(image_square, 0.0) + epsilon)
    scale = scale_first / norm_image
    stores = [
        pltpu.make_async_copy(source, result, store_sem.at[n])
        for n, (source, result) in enumerate(
            zip((basis_out, remainder_out, hessenberg_out), results)
        )
    ]
    for l in range(leaves):
        basis = (image[l] + shift * vector[l]) * scale
        basis_out[l] = basis
        remainder_out[l] = 0.5 * basis + (image_two[l] + shift * image[l]) * scale
    start_sums(
        products(
            [
                (vector, remainder_out),
                (basis_out, remainder_out),
                (remainder_out, remainder_out),
                (basis_out, vector),
                (basis_out, basis_out),
            ]
        )
    )
    stores[0].start()
    drain(0, field_a, coef_a, group_a)
    first_with, basis_with, square_two, cross_term, basis_square = finish_sums(5)
    first_with = first_with * scale_first
    cross_term = cross_term * scale_first
    proj_basis = basis_with - first_with * cross_term
    first_part = first_with * scale_first
    for l in range(leaves):
        remainder_out[l] = (
            remainder_out[l] - first_part * vector[l] - proj_basis * basis_out[l]
        )
    stores[1].start()
    last_square = (
        square_two
        + first_with * first_with * first_square
        + proj_basis * proj_basis * basis_square
        - 2.0 * first_with * first_with
        - 2.0 * proj_basis * basis_with
        + 2.0 * first_with * proj_basis * cross_term
    )
    norm_last = jnp.sqrt(jnp.maximum(last_square, 0.0) + epsilon)
    for n, entry in enumerate([proj_first, norm_image, first_with, proj_basis, norm_last]):
        line = jnp.sum(jnp.where(lane_at == sub_at, entry, 0.0), axis=0, keepdims=True)
        hessenberg_out[n : n + 1, :] = line[:, :rhs]
    stores[2].start()
    drain(1, field_b, coef_b, group_b)
    if grp > 1:
        wait_bytes(sums_a.at[pl.ds(0, grp - 1)], sums_send.at[0])
    if rows > 1:
        wait_bytes(sums_b.at[pl.ds(0, rows - 1)], sums_send.at[1])
    for store in stores:
        store.wait()


def hand_on(*refs):
    sources, results, places, load_sem, store_sem = refs[:3], refs[3:6], refs[6:9], refs[9], refs[10]
    loads = [pltpu.make_async_copy(sources[n], places[n], load_sem.at[n]) for n in range(3)]
    stores = [pltpu.make_async_copy(places[n], results[n], store_sem.at[n]) for n in range(3)]
    for load in loads:
        load.start()
    for load, store in zip(loads, stores):
        load.wait()
        store.start()
    for store in stores:
        store.wait()


def shards(
    rows,
    grp,
    vector,
    near_cols,
    near_blocks,
    col_basis,
    row_basis,
    leaf_far,
    leaf_coupling,
    leaf_transfer,
    box_far,
    box_coupling,
    box_transfer,
    coarse_far,
    coarse_coupling,
):
    leaves, rhs, cells = vector.shape
    rank = col_basis.shape[1]
    assert leaves * rank == LANES and box_far.shape[0] == 1 and coarse_far.shape[0] == 1
    assert 5 * rhs <= LANES and 2 * rank + 9 <= LANES and rank & (rank - 1) == 0
    hbm = pl.BlockSpec(memory_space=pltpu.HBM)
    slots = max(leaf_far.shape[1], box_far.shape[1], coarse_far.shape[1])
    dma = pltpu.SemaphoreType.DMA
    operands = (
        near_cols,
        leaf_far,
        box_far,
        coarse_far,
        vector,
        near_blocks,
        col_basis,
        row_basis,
        leaf_coupling,
        leaf_transfer,
        box_coupling,
        box_transfer,
        coarse_coupling,
    )
    shapes = (
        jax.ShapeDtypeStruct(vector.shape, f32),
        jax.ShapeDtypeStruct(vector.shape, f32),
        jax.ShapeDtypeStruct((5, rhs), f32),
    )
    results = pl.pallas_call(
        functools.partial(kernel, rows, grp),
        out_shape=shapes,
        in_specs=[hbm] * len(operands),
        out_specs=(hbm, hbm, hbm),
        scratch_shapes=[
            *[pltpu.SMEM(operand.shape, operand.dtype) for operand in operands[:4]],
            *[pltpu.VMEM(operand.shape, operand.dtype) for operand in operands[4:]],
            pltpu.VMEM((3 * leaves, rhs, cells), bf16),
            pltpu.VMEM((3 * leaves, rhs, cells), bf16),
            pltpu.VMEM((3 * grp, 2, rhs, LANES), bf16),
            pltpu.VMEM((3 * grp, 2, rhs, LANES), bf16),
            pltpu.VMEM((rows, rhs, LANES), bf16),
            pltpu.VMEM((rows, rhs, LANES), bf16),
            pltpu.VMEM((grp, 1, LANES), f32),
            pltpu.VMEM((rows, 1, LANES), f32),
            pltpu.VMEM((2 * LANES, leaves * cells), bf16),
            pltpu.VMEM((LANES, leaves * cells), bf16),
            pltpu.VMEM((leaves, rank, leaf_far.shape[1] * LANES), bf16),
            pltpu.VMEM((LANES, box_far.shape[1] * LANES), bf16),
            pltpu.VMEM((LANES, coarse_far.shape[1] * LANES), bf16),
            pltpu.VMEM(vector.shape, f32),
            pltpu.VMEM(vector.shape, f32),
            pltpu.VMEM((slots * rank, slots * LANES), bf16),
            pltpu.VMEM(vector.shape, f32),
            pltpu.VMEM(vector.shape, f32),
            pltpu.VMEM((5, rhs), f32),
            dma((3,)),
            dma((len(operands),)),
            dma((2, 2)),
            dma((2, 2)),
            dma((2, 3)),
            dma((2, 3)),
            dma((2,)),
            dma((2,)),
            dma((2,)),
            dma((2,)),
        ],
        compiler_params=pltpu.CompilerParams(
            collective_id=0, has_side_effects=True, vmem_limit_bytes=65100 * 1024
        ),
    )(*operands)
    basis, remainder, entries = pl.pallas_call(
        hand_on,
        out_shape=shapes,
        in_specs=[hbm] * 3,
        out_specs=(hbm, hbm, hbm),
        scratch_shapes=[pltpu.VMEM(shape.shape, f32) for shape in shapes] + [dma((3,))] * 2,
        compiler_params=pltpu.CompilerParams(vmem_limit_bytes=65100 * 1024),
    )(*results)
    return basis, remainder, entries.T


def solution(mesh):
    return jax.shard_map(
        functools.partial(shards, mesh.shape["rows"], mesh.shape["grp"]),
        mesh=mesh,
        in_specs=(
            P(("rows", "grp"), None, None),
            P(("rows", "grp"), None),
            P(("rows", "grp"), None, None, None),
            P(("rows", "grp"), None, None),
            P(("rows", "grp"), None, None),
            P(("rows", "grp"), None),
            P(("rows", "grp"), None, None),
            P(("rows", "grp"), None, None),
            P(("rows", "grp"), None),
            P(("rows", "grp"), None, None),
            P(("rows", "grp"), None, None),
            P("rows", None),
            P("rows", None, None),
        ),
        out_specs=(P(("rows", "grp"), None, None), P(("rows", "grp"), None, None), P()),
        check_vma=False,
    )
```

```python
import functools

import jax
import jax.numpy as jnp
from jax import lax
from jax.experimental import pallas as pl
from jax.experimental.pallas import tpu as pltpu
from jax.sharding import PartitionSpec as P

LANES = 128
epsilon = 1e-06
highest = lax.Precision.HIGHEST
MESH = pl.DeviceIdType.MESH
bf16 = jnp.bfloat16
f32 = jnp.float32


def nt(left, right, precision=None):
    return lax.dot_general(
        left, right, (((1,), (1,)), ((), ())), precision=precision, preferred_element_type=f32
    )


def wrap(index, size):
    return jnp.where(index >= size, index - size, index)


def kernel(
    rows,
    grp,
    *refs,
):
    sources = refs[:13]
    results = refs[13:16]
    targets = refs[16:29]
    (
        near_cols,
        leaf_far,
        box_far,
        coarse_far,
        vector,
        near_blocks,
        col_basis,
        row_basis,
        leaf_coupling,
        leaf_transfer,
        box_coupling,
        box_transfer,
        coarse_coupling,
    ) = targets
    (
        field_a,
        field_b,
        coef_a,
        coef_b,
        group_a,
        group_b,
        sums,
        send_basis,
        receive_basis,
        leaf_weights,
        box_weights,
        group_weights,
        image,
        image_two,
        picked,
        select,
        basis_out,
        remainder_out,
        hessenberg_out,
        store_sem,
        load_sem,
        field_send,
        field_recv,
        coef_send,
        coef_recv,
        group_send,
        group_recv,
        sums_send,
        sums_recv,
    ) = refs[29:]
    leaves, rhs, cells = vector.shape
    rank = col_basis.shape[1]
    near_count = near_cols.shape[1]
    leaf_slots = leaf_far.shape[1]
    box_slots = box_far.shape[1]
    coarse_slots = coarse_far.shape[1]
    devices = rows * grp
    total_count = leaves * devices * cells
    row = lax.axis_index("rows")
    z = lax.axis_index("grp")
    me = row * grp + z

    loads = [
        pltpu.make_async_copy(source, target, load_sem.at[n])
        for n, (source, target) in enumerate(zip(sources, targets))
    ]
    for n in (4, 6, 9, 11, 7, 8, 10, 12, 0, 1, 2, 3, 5):
        loads[n].start()

    barrier = pltpu.get_barrier_semaphore()

    def each_other(visit):
        def one_row(step, carry):
            to_row = wrap(row + step, rows)
            for turn in range(grp):
                visit(to_row, wrap(z + turn, grp))
            return carry

        for turn in range(1, grp):
            visit(row, wrap(z + turn, grp))
        lax.fori_loop(1, rows, one_row, 0)

    def greet(to_row, to_z):
        pl.semaphore_signal(barrier, inc=1, device_id=(to_row, to_z), device_id_type=MESH)

    each_other(greet)

    send_basis[...] = jnp.zeros_like(send_basis)
    picked[...] = jnp.zeros_like(picked)
    for n in (4, 6, 9, 11):
        loads[n].wait()
    for l in range(leaves):
        send_basis[l * rank : (l + 1) * rank, l * cells : (l + 1) * cells] = col_basis[l]
    width = leaves * rank
    transfer = leaf_transfer[...].reshape(width, rank)
    down = jnp.dot(transfer, box_transfer[0], precision=highest, preferred_element_type=f32)
    up = jnp.concatenate([transfer, down], axis=1).T
    up_high = up.astype(bf16)
    up_low = (up - up_high.astype(f32)).astype(bf16)
    plain = send_basis[:width]
    send_basis[width : width + 2 * rank] = (
        jnp.dot(up_high, plain, preferred_element_type=f32)
        + jnp.dot(up_low, plain, preferred_element_type=f32)
    ).astype(bf16)

    def prepare_receive():
        for n in (7, 8, 10, 12, 0, 1, 2, 3):
            loads[n].wait()
        receive_basis[...] = jnp.zeros_like(receive_basis)
        for l in range(leaves):
            receive_basis[l * rank : (l + 1) * rank, l * cells : (l + 1) * cells] = row_basis[l]
        lane = lax.broadcasted_iota(jnp.int32, (rank, LANES), 1)
        unit = lax.broadcasted_iota(jnp.int32, (rank, LANES), 0)
        select[...] = jnp.zeros_like(select)
        for k in range(select.shape[0] // rank):
            select[k * rank : (k + 1) * rank, k * LANES : (k + 1) * LANES] = jnp.where(
                (lane & (rank - 1)) == unit, 1.0, 0.0
            ).astype(bf16)
        tiled = jnp.dot(
            leaf_coupling[...].reshape(width, leaf_slots * rank),
            select[: leaf_slots * rank, : leaf_slots * LANES],
            preferred_element_type=f32,
        )
        for l in range(leaves):
            for k in range(leaf_slots):
                start = lax.rem(leaf_far[l, k], leaves) * rank
                piece = tiled[l * rank : (l + 1) * rank, k * LANES : (k + 1) * LANES]
                leaf_weights[l, :, k * LANES : (k + 1) * LANES] = jnp.where(
                    (lane >= start) & (lane < start + rank), piece, 0.0
                ).astype(bf16)

        def compose(target, coupling, above, low):
            slots = coupling.shape[1] // rank
            wide = jnp.dot(
                coupling, select[: slots * rank, : slots * LANES], preferred_element_type=f32
            )
            place = lax.broadcasted_iota(jnp.int32, wide.shape, 1) & (LANES - 1)
            wide = jnp.where((place >= low) & (place < low + rank), wide, 0.0).astype(bf16)
            above_high = above.astype(bf16)
            above_low = (above - above_high.astype(f32)).astype(bf16)
            target[...] = (
                jnp.dot(above_high, wide, preferred_element_type=f32)
                + jnp.dot(above_low, wide, preferred_element_type=f32)
            ).astype(bf16)

        compose(box_weights, box_coupling[0], transfer, 0)
        compose(group_weights, coarse_coupling[0], down, rank)

    def send(src, dst, send_sem, recv_sem, to_row, to_z):
        pltpu.make_async_remote_copy(
            src_ref=src,
            dst_ref=dst,
            send_sem=send_sem,
            recv_sem=recv_sem,
            device_id=(to_row, to_z),
            device_id_type=MESH,
        ).start()

    def wait_bytes(ref, sem):
        pltpu.make_async_copy(ref, ref, sem).wait()

    def near_product(result, start, stop, pick, add):
        total = None
        for l in range(leaves):
            for k in range(start, stop):
                picked[l, k, l * rhs : (l + 1) * rhs] = pick(l, k)
                product = nt(near_blocks[l, k], picked[l, k])
                total = product if total is None else total + product
        turned = total.T
        for l in range(leaves):
            rows_of = turned[l * rhs : (l + 1) * rhs]
            result[l] = result[l] + rows_of if add else rows_of

    sub_at = lax.broadcasted_iota(jnp.int32, (rhs, LANES), 0)
    lane_at = lax.broadcasted_iota(jnp.int32, (rhs, LANES), 1)

    def with_sums(tile, columns):
        for n, column in enumerate(columns):
            for part in range(3):
                piece = column.astype(bf16).astype(f32)
                tile = jnp.where(lane_at == 2 * rank + 3 * n + part, piece, tile)
                column = column - piece
        return tile

    def read_sums(tile, count):
        return [
            jnp.sum(
                jnp.where(
                    (lane_at >= 2 * rank + 3 * n) & (lane_at < 2 * rank + 3 * n + 3), tile, 0.0
                ),
                axis=1,
                keepdims=True,
            )
            for n in range(count)
        ]

    def operator(phase, source, result, field, coef, group, own_sums, after_send, before_near):
        for l in range(leaves):
            field[leaves + l] = source[l].astype(bf16)
        if phase == 0:
            pl.semaphore_wait(barrier, devices - 1)
        own = field.at[pl.ds(leaves, leaves)]
        low = field.at[pl.ds(0, leaves)]
        high = field.at[pl.ds(2 * leaves, leaves)]

        @pl.when(me < devices - 1)
        def _():
            last = z == grp - 1
            send(
                own,
                low,
                field_send.at[phase, 0],
                field_recv.at[phase, 0],
                jnp.where(last, row + 1, row),
                jnp.where(last, 0, z + 1),
            )

        @pl.when(me > 0)
        def _():
            send(
                own,
                high,
                field_send.at[phase, 1],
                field_recv.at[phase, 1],
                jnp.where(z == 0, row - 1, row),
                jnp.where(z == 0, grp - 1, z - 1),
            )

        wide = jnp.concatenate([field[leaves + l] for l in range(leaves)], axis=1)
        sent = nt(wide, send_basis[...])
        mine = grp + z
        coef[mine, 0] = sent[:, :LANES].astype(bf16)
        coef[mine, 1] = with_sums(sent[:, LANES:], own_sums()).astype(bf16)

        for step in range(1, grp):
            send(
                coef.at[mine],
                coef.at[mine],
                coef_send.at[phase, 1],
                coef_recv.at[phase, 1],
                row,
                wrap(z + step, grp),
            )

        @pl.when(row > 0)
        def _():
            for other in range(grp):
                send(
                    coef.at[mine],
                    coef.at[2 * grp + z],
                    coef_send.at[phase, 0],
                    coef_recv.at[phase, 2],
                    row - 1,
                    other,
                )

        @pl.when(row < rows - 1)
        def _():
            for other in range(grp):
                send(
                    coef.at[mine],
                    coef.at[z],
                    coef_send.at[phase, 2],
                    coef_recv.at[phase, 0],
                    row + 1,
                    other,
                )

        after_send()
        before_near()
        near_product(result, 0, 1, lambda l, k: field[leaves + l], False)

        if grp > 1:
            wait_bytes(coef.at[pl.ds(0, grp - 1)], coef_recv.at[phase, 1])
        together = coef[grp, 1].astype(f32)
        for other in range(1, grp):
            together = together + coef[grp + other, 1].astype(f32)
        if phase == 1:
            together = with_sums(together, read_sums(together, 3))
        group[row] = together.astype(bf16)

        def send_group(step, carry):
            send(
                group.at[row],
                group.at[row],
                group_send.at[phase],
                group_recv.at[phase],
                wrap(row + step, rows),
                z,
            )
            return carry

        lax.fori_loop(1, rows, send_group, 0)

        @pl.when(me > 0)
        def _():
            wait_bytes(low, field_recv.at[phase, 0])

        @pl.when(me < devices - 1)
        def _():
            wait_bytes(high, field_recv.at[phase, 1])

        first = me * leaves - leaves

        def pick(l, k):
            return field[jnp.clip(near_cols[l, k] - first, 0, 3 * leaves - 1)]

        near_product(result, 1, near_count, pick, True)

        @pl.when(row > 0)
        def _():
            wait_bytes(coef.at[pl.ds(0, grp)], coef_recv.at[phase, 0])

        @pl.when(row < rows - 1)
        def _():
            wait_bytes(coef.at[pl.ds(0, grp)], coef_recv.at[phase, 2])

        def slot(box):
            return jnp.clip(box - (row * grp - grp), 0, 3 * grp - 1)

        parts = []
        for l in range(leaves):
            taken = jnp.concatenate(
                [
                    coef[slot(lax.div(leaf_far[l, k], leaves)), 0]
                    for k in range(leaf_slots)
                ],
                axis=1,
            )
            parts.append(nt(taken, leaf_weights[l]))
        local = jnp.concatenate(parts, axis=1)
        taken = jnp.concatenate(
            [coef[slot(box_far[0, k]), 1] for k in range(box_slots)], axis=1
        )
        local = local + nt(taken, box_weights[...])
        if rows > 1:
            wait_bytes(group.at[pl.ds(0, rows - 1)], group_recv.at[phase])
        taken = jnp.concatenate([group[coarse_far[0, k]] for k in range(coarse_slots)], axis=1)
        local = local + nt(taken, group_weights[...])
        far = jnp.dot(local.astype(bf16), receive_basis[...], preferred_element_type=f32)
        for l in range(leaves):
            result[l] = result[l] + far[:, l * cells : (l + 1) * cells]

    def drain(phase, field, coef, group):
        own = field.at[pl.ds(leaves, leaves)]

        @pl.when(me < devices - 1)
        def _():
            wait_bytes(own, field_send.at[phase, 0])

        @pl.when(me > 0)
        def _():
            wait_bytes(own, field_send.at[phase, 1])

        @pl.when(row > 0)
        def _():
            wait_bytes(coef.at[pl.ds(0, grp)], coef_send.at[phase, 0])

        if grp > 1:
            wait_bytes(coef.at[pl.ds(0, grp - 1)], coef_send.at[phase, 1])

        @pl.when(row < rows - 1)
        def _():
            wait_bytes(coef.at[pl.ds(0, grp)], coef_send.at[phase, 2])

        if rows > 1:
            wait_bytes(group.at[pl.ds(0, rows - 1)], group_send.at[phase])

    def start_sums(columns):
        spread = jnp.zeros((rhs, LANES), f32)
        for n, column in enumerate(columns):
            spread = jnp.where(lane_at == sub_at + n * rhs, column, spread)
        sums[me] = jnp.sum(spread, axis=0, keepdims=True)

        def send_sums(to_row, to_z):
            send(sums.at[me], sums.at[me], sums_send, sums_recv, to_row, to_z)

        each_other(send_sums)

    def finish_sums(count):
        wait_bytes(sums.at[pl.ds(0, devices - 1)], sums_recv)
        line = jnp.sum(sums[...], axis=0) / total_count
        spread = jnp.broadcast_to(line, (rhs, LANES))
        return [
            jnp.sum(jnp.where(lane_at == sub_at + n * rhs, spread, 0.0), axis=1, keepdims=True)
            for n in range(count)
        ]

    def products(pairs):
        columns = []
        for left, right in pairs:
            total = left[0] * right[0]
            for l in range(1, leaves):
                total = total + left[l] * right[l]
            columns.append(jnp.sum(total, axis=1, keepdims=True))
        return columns

    def first_sums():
        return products([(vector, vector), (vector, image), (image, image)])

    operator(
        0,
        vector,
        image,
        field_a,
        coef_a,
        group_a,
        lambda: [],
        prepare_receive,
        loads[5].wait,
    )
    operator(
        1,
        image,
        image_two,
        field_b,
        coef_b,
        group_b,
        first_sums,
        lambda: None,
        lambda: None,
    )

    together = group_b[0].astype(f32)
    for n in range(1, rows):
        together = together + group_b[n].astype(f32)
    vv, vu, uu = [column / total_count for column in read_sums(together, 3)]
    norm_first = jnp.sqrt(vv + epsilon)
    scale_first = 1.0 / norm_first
    first_square = vv * scale_first * scale_first
    proj_first = (0.5 * vv + vu) * scale_first * scale_first
    shift = 0.5 - proj_first
    image_square = (uu + 2.0 * shift * vu + shift * shift * vv) * scale_first * scale_first
    norm_image = jnp.sqrt(jnp.maximum(image_square, 0.0) + epsilon)
    scale = scale_first / norm_image
    stores = [
        pltpu.make_async_copy(source, result, store_sem.at[n])
        for n, (source, result) in enumerate(
            zip((basis_out, remainder_out, hessenberg_out), results)
        )
    ]
    for l in range(leaves):
        basis = (image[l] + shift * vector[l]) * scale
        basis_out[l] = basis
        remainder_out[l] = 0.5 * basis + (image_two[l] + shift * image[l]) * scale
    start_sums(
        products(
            [
                (vector, remainder_out),
                (basis_out, remainder_out),
                (remainder_out, remainder_out),
                (basis_out, vector),
                (basis_out, basis_out),
            ]
        )
    )
    stores[0].start()
    drain(0, field_a, coef_a, group_a)
    first_with, basis_with, square_two, cross_term, basis_square = finish_sums(5)
    first_with = first_with * scale_first
    cross_term = cross_term * scale_first
    proj_basis = basis_with - first_with * cross_term
    first_part = first_with * scale_first
    for l in range(leaves):
        remainder_out[l] = (
            remainder_out[l] - first_part * vector[l] - proj_basis * basis_out[l]
        )
    stores[1].start()
    last_square = (
        square_two
        + first_with * first_with * first_square
        + proj_basis * proj_basis * basis_square
        - 2.0 * first_with * first_with
        - 2.0 * proj_basis * basis_with
        + 2.0 * first_with * proj_basis * cross_term
    )
    norm_last = jnp.sqrt(jnp.maximum(last_square, 0.0) + epsilon)
    for n, entry in enumerate([proj_first, norm_image, first_with, proj_basis, norm_last]):
        line = jnp.sum(jnp.where(lane_at == sub_at, entry, 0.0), axis=0, keepdims=True)
        hessenberg_out[n : n + 1, :] = line[:, :rhs]
    stores[2].start()
    drain(1, field_b, coef_b, group_b)
    wait_bytes(sums.at[pl.ds(0, devices - 1)], sums_send)
    for store in stores:
        store.wait()


def hand_on(*refs):
    sources, results, places, load_sem, store_sem = refs[:3], refs[3:6], refs[6:9], refs[9], refs[10]
    loads = [pltpu.make_async_copy(sources[n], places[n], load_sem.at[n]) for n in range(3)]
    stores = [pltpu.make_async_copy(places[n], results[n], store_sem.at[n]) for n in range(3)]
    for load in loads:
        load.start()
    for load, store in zip(loads, stores):
        load.wait()
        store.start()
    for store in stores:
        store.wait()


def shards(
    rows,
    grp,
    vector,
    near_cols,
    near_blocks,
    col_basis,
    row_basis,
    leaf_far,
    leaf_coupling,
    leaf_transfer,
    box_far,
    box_coupling,
    box_transfer,
    coarse_far,
    coarse_coupling,
):
    leaves, rhs, cells = vector.shape
    rank = col_basis.shape[1]
    assert leaves * rank == LANES and box_far.shape[0] == 1 and coarse_far.shape[0] == 1
    assert 5 * rhs <= LANES and 2 * rank + 9 <= LANES and rank & (rank - 1) == 0
    hbm = pl.BlockSpec(memory_space=pltpu.HBM)
    slots = max(leaf_far.shape[1], box_far.shape[1], coarse_far.shape[1])
    dma = pltpu.SemaphoreType.DMA
    operands = (
        near_cols,
        leaf_far,
        box_far,
        coarse_far,
        vector,
        near_blocks,
        col_basis,
        row_basis,
        leaf_coupling,
        leaf_transfer,
        box_coupling,
        box_transfer,
        coarse_coupling,
    )
    shapes = (
        jax.ShapeDtypeStruct(vector.shape, f32),
        jax.ShapeDtypeStruct(vector.shape, f32),
        jax.ShapeDtypeStruct((5, rhs), f32),
    )
    results = pl.pallas_call(
        functools.partial(kernel, rows, grp),
        out_shape=shapes,
        in_specs=[hbm] * len(operands),
        out_specs=(hbm, hbm, hbm),
        scratch_shapes=[
            *[pltpu.SMEM(operand.shape, operand.dtype) for operand in operands[:4]],
            *[pltpu.VMEM(operand.shape, operand.dtype) for operand in operands[4:]],
            pltpu.VMEM((3 * leaves, rhs, cells), bf16),
            pltpu.VMEM((3 * leaves, rhs, cells), bf16),
            pltpu.VMEM((3 * grp, 2, rhs, LANES), bf16),
            pltpu.VMEM((3 * grp, 2, rhs, LANES), bf16),
            pltpu.VMEM((rows, rhs, LANES), bf16),
            pltpu.VMEM((rows, rhs, LANES), bf16),
            pltpu.VMEM((rows * grp, 1, LANES), f32),
            pltpu.VMEM((2 * LANES, leaves * cells), bf16),
            pltpu.VMEM((LANES, leaves * cells), bf16),
            pltpu.VMEM((leaves, rank, leaf_far.shape[1] * LANES), bf16),
            pltpu.VMEM((LANES, box_far.shape[1] * LANES), bf16),
            pltpu.VMEM((LANES, coarse_far.shape[1] * LANES), bf16),
            pltpu.VMEM(vector.shape, f32),
            pltpu.VMEM(vector.shape, f32),
            pltpu.VMEM((*near_blocks.shape[:2], leaves * rhs, cells), bf16),
            pltpu.VMEM((slots * rank, slots * LANES), bf16),
            pltpu.VMEM(vector.shape, f32),
            pltpu.VMEM(vector.shape, f32),
            pltpu.VMEM((5, rhs), f32),
            dma((3,)),
            dma((len(operands),)),
            dma((2, 2)),
            dma((2, 2)),
            dma((2, 3)),
            dma((2, 3)),
            dma((2,)),
            dma((2,)),
            dma(()),
            dma(()),
        ],
        compiler_params=pltpu.CompilerParams(
            collective_id=0, has_side_effects=True, vmem_limit_bytes=65100 * 1024
        ),
    )(*operands)
    basis, remainder, entries = pl.pallas_call(
        hand_on,
        out_shape=shapes,
        in_specs=[hbm] * 3,
        out_specs=(hbm, hbm, hbm),
        scratch_shapes=[pltpu.VMEM(shape.shape, f32) for shape in shapes] + [dma((3,))] * 2,
        compiler_params=pltpu.CompilerParams(vmem_limit_bytes=65100 * 1024),
    )(*results)
    return basis, remainder, entries.T


def solution(mesh):
    return jax.shard_map(
        functools.partial(shards, mesh.shape["rows"], mesh.shape["grp"]),
        mesh=mesh,
        in_specs=(
            P(("rows", "grp"), None, None),
            P(("rows", "grp"), None),
            P(("rows", "grp"), None, None, None),
            P(("rows", "grp"), None, None),
            P(("rows", "grp"), None, None),
            P(("rows", "grp"), None),
            P(("rows", "grp"), None, None),
            P(("rows", "grp"), None, None),
            P(("rows", "grp"), None),
            P(("rows", "grp"), None, None),
            P(("rows", "grp"), None, None),
            P("rows", None),
            P("rows", None, None),
        ),
        out_specs=(P(("rows", "grp"), None, None), P(("rows", "grp"), None, None), P()),
        check_vma=False,
    )
```

```python
import functools

import jax
import jax.numpy as jnp
from jax import lax
from jax.experimental import pallas as pl
from jax.experimental.pallas import tpu as pltpu
from jax.sharding import PartitionSpec as P

LANES = 128
epsilon = 1e-06
highest = lax.Precision.HIGHEST
MESH = pl.DeviceIdType.MESH
bf16 = jnp.bfloat16
f32 = jnp.float32


def nt(left, right, precision=None):
    return lax.dot_general(
        left, right, (((1,), (1,)), ((), ())), precision=precision, preferred_element_type=f32
    )


def wrap(index, size):
    return jnp.where(index >= size, index - size, index)


def kernel(
    rows,
    grp,
    *refs,
):
    sources = refs[:13]
    results = refs[13:16]
    targets = refs[16:29]
    (
        near_cols,
        leaf_far,
        box_far,
        coarse_far,
        vector,
        near_blocks,
        col_basis,
        row_basis,
        leaf_coupling,
        leaf_transfer,
        box_coupling,
        box_transfer,
        coarse_coupling,
    ) = targets
    (
        field_a,
        field_b,
        coef_a,
        coef_b,
        group_a,
        group_b,
        sums,
        send_basis,
        receive_basis,
        leaf_weights,
        box_weights,
        group_weights,
        image,
        image_two,
        picked,
        select,
        basis_out,
        remainder_out,
        hessenberg_out,
        store_sem,
        load_sem,
        field_send,
        field_recv,
        coef_send,
        coef_recv,
        group_send,
        group_recv,
        sums_send,
        sums_recv,
    ) = refs[29:]
    leaves, rhs, cells = vector.shape
    rank = col_basis.shape[1]
    near_count = near_cols.shape[1]
    leaf_slots = leaf_far.shape[1]
    box_slots = box_far.shape[1]
    coarse_slots = coarse_far.shape[1]
    devices = rows * grp
    total_count = leaves * devices * cells
    row = lax.axis_index("rows")
    z = lax.axis_index("grp")
    me = row * grp + z

    loads = [
        pltpu.make_async_copy(source, target, load_sem.at[n])
        for n, (source, target) in enumerate(zip(sources, targets))
    ]
    for n in (4, 6, 9, 11, 7, 8, 10, 12, 0, 1, 2, 3, 5):
        loads[n].start()

    barrier = pltpu.get_barrier_semaphore()

    def each_other(visit):
        def one_row(step, carry):
            to_row = wrap(row + step, rows)
            for turn in range(grp):
                visit(to_row, wrap(z + turn, grp))
            return carry

        for turn in range(1, grp):
            visit(row, wrap(z + turn, grp))
        lax.fori_loop(1, rows, one_row, 0)

    def greet(to_row, to_z):
        pl.semaphore_signal(barrier, inc=1, device_id=(to_row, to_z), device_id_type=MESH)

    each_other(greet)

    send_basis[...] = jnp.zeros_like(send_basis)
    picked[...] = jnp.zeros_like(picked)
    for n in (4, 6, 9, 11):
        loads[n].wait()
    for l in range(leaves):
        send_basis[l * rank : (l + 1) * rank, l * cells : (l + 1) * cells] = col_basis[l]
    width = leaves * rank
    transfer = leaf_transfer[...].reshape(width, rank)
    down = jnp.dot(transfer, box_transfer[0], precision=highest, preferred_element_type=f32)
    up = jnp.concatenate([transfer, down], axis=1).T
    up_high = up.astype(bf16)
    up_low = (up - up_high.astype(f32)).astype(bf16)
    plain = send_basis[:width]
    send_basis[width : width + 2 * rank] = (
        jnp.dot(up_high, plain, preferred_element_type=f32)
        + jnp.dot(up_low, plain, preferred_element_type=f32)
    ).astype(bf16)

    def prepare_receive():
        for n in (7, 8, 10, 12, 0, 1, 2, 3):
            loads[n].wait()
        receive_basis[...] = jnp.zeros_like(receive_basis)
        for l in range(leaves):
            receive_basis[l * rank : (l + 1) * rank, l * cells : (l + 1) * cells] = row_basis[l]
        lane = lax.broadcasted_iota(jnp.int32, (rank, LANES), 1)
        unit = lax.broadcasted_iota(jnp.int32, (rank, LANES), 0)
        select[...] = jnp.zeros_like(select)
        for k in range(select.shape[0] // rank):
            select[k * rank : (k + 1) * rank, k * LANES : (k + 1) * LANES] = jnp.where(
                (lane & (rank - 1)) == unit, 1.0, 0.0
            ).astype(bf16)
        tiled = jnp.dot(
            leaf_coupling[...].reshape(width, leaf_slots * rank),
            select[: leaf_slots * rank, : leaf_slots * LANES],
            preferred_element_type=f32,
        )
        for l in range(leaves):
            for k in range(leaf_slots):
                start = lax.rem(leaf_far[l, k], leaves) * rank
                piece = tiled[l * rank : (l + 1) * rank, k * LANES : (k + 1) * LANES]
                leaf_weights[l, :, k * LANES : (k + 1) * LANES] = jnp.where(
                    (lane >= start) & (lane < start + rank), piece, 0.0
                ).astype(bf16)

        def compose(target, coupling, above, low):
            slots = coupling.shape[1] // rank
            wide = jnp.dot(
                coupling, select[: slots * rank, : slots * LANES], preferred_element_type=f32
            )
            place = lax.broadcasted_iota(jnp.int32, wide.shape, 1) & (LANES - 1)
            wide = jnp.where((place >= low) & (place < low + rank), wide, 0.0).astype(bf16)
            above_high = above.astype(bf16)
            above_low = (above - above_high.astype(f32)).astype(bf16)
            target[...] = (
                jnp.dot(above_high, wide, preferred_element_type=f32)
                + jnp.dot(above_low, wide, preferred_element_type=f32)
            ).astype(bf16)

        compose(box_weights, box_coupling[0], transfer, 0)
        compose(group_weights, coarse_coupling[0], down, rank)

    def send(src, dst, send_sem, recv_sem, to_row, to_z):
        pltpu.make_async_remote_copy(
            src_ref=src,
            dst_ref=dst,
            send_sem=send_sem,
            recv_sem=recv_sem,
            device_id=(to_row, to_z),
            device_id_type=MESH,
        ).start()

    def wait_bytes(ref, sem):
        pltpu.make_async_copy(ref, ref, sem).wait()

    def near_product(result, start, stop, pick, add):
        total = None
        for l in range(leaves):
            for k in range(start, stop):
                picked[l, k, l * rhs : (l + 1) * rhs] = pick(l, k)
                product = nt(near_blocks[l, k], picked[l, k])
                total = product if total is None else total + product
        turned = total.T
        for l in range(leaves):
            rows_of = turned[l * rhs : (l + 1) * rhs]
            result[l] = result[l] + rows_of if add else rows_of

    sub_at = lax.broadcasted_iota(jnp.int32, (rhs, LANES), 0)
    lane_at = lax.broadcasted_iota(jnp.int32, (rhs, LANES), 1)

    def with_sums(tile, columns):
        for n, column in enumerate(columns):
            for part in range(3):
                piece = column.astype(bf16).astype(f32)
                tile = jnp.where(lane_at == 2 * rank + 3 * n + part, piece, tile)
                column = column - piece
        return tile

    def read_sums(tile, count):
        return [
            jnp.sum(
                jnp.where(
                    (lane_at >= 2 * rank + 3 * n) & (lane_at < 2 * rank + 3 * n + 3), tile, 0.0
                ),
                axis=1,
                keepdims=True,
            )
            for n in range(count)
        ]

    def operator(phase, source, result, field, coef, group, own_sums, after_send, before_near):
        for l in range(leaves):
            field[leaves + l] = source[l].astype(bf16)
        if phase == 0:
            pl.semaphore_wait(barrier, devices - 1)
        own = field.at[pl.ds(leaves, leaves)]
        low = field.at[pl.ds(0, leaves)]
        high = field.at[pl.ds(2 * leaves, leaves)]

        wide = jnp.concatenate([field[leaves + l] for l in range(leaves)], axis=1)
        sent = nt(wide, send_basis[...])
        mine = grp + z
        coef[mine, 0] = sent[:, :LANES].astype(bf16)
        coef[mine, 1] = with_sums(sent[:, LANES:], own_sums()).astype(bf16)

        for step in range(1, grp):
            send(
                coef.at[mine],
                coef.at[mine],
                coef_send.at[phase, 1],
                coef_recv.at[phase, 1],
                row,
                wrap(z + step, grp),
            )

        @pl.when(me < devices - 1)
        def _():
            last = z == grp - 1
            send(
                own,
                low,
                field_send.at[phase, 0],
                field_recv.at[phase, 0],
                jnp.where(last, row + 1, row),
                jnp.where(last, 0, z + 1),
            )

        @pl.when(me > 0)
        def _():
            send(
                own,
                high,
                field_send.at[phase, 1],
                field_recv.at[phase, 1],
                jnp.where(z == 0, row - 1, row),
                jnp.where(z == 0, grp - 1, z - 1),
            )

        after_send()
        before_near()
        near_product(result, 0, 1, lambda l, k: field[leaves + l], False)

        if grp > 1:
            wait_bytes(coef.at[pl.ds(0, grp - 1)], coef_recv.at[phase, 1])
        whole_row = coef.at[pl.ds(grp, grp)]

        @pl.when(row > 0)
        def _():
            send(
                whole_row,
                coef.at[pl.ds(2 * grp, grp)],
                coef_send.at[phase, 0],
                coef_recv.at[phase, 2],
                row - 1,
                z,
            )

        @pl.when(row < rows - 1)
        def _():
            send(
                whole_row,
                coef.at[pl.ds(0, grp)],
                coef_send.at[phase, 2],
                coef_recv.at[phase, 0],
                row + 1,
                z,
            )

        together = coef[grp, 1].astype(f32)
        for other in range(1, grp):
            together = together + coef[grp + other, 1].astype(f32)
        if phase == 1:
            together = with_sums(together, read_sums(together, 3))
        group[row] = together.astype(bf16)

        def send_group(step, carry):
            send(
                group.at[row],
                group.at[row],
                group_send.at[phase],
                group_recv.at[phase],
                wrap(row + step, rows),
                z,
            )
            return carry

        lax.fori_loop(1, rows, send_group, 0)

        @pl.when(me > 0)
        def _():
            wait_bytes(low, field_recv.at[phase, 0])

        @pl.when(me < devices - 1)
        def _():
            wait_bytes(high, field_recv.at[phase, 1])

        first = me * leaves - leaves

        def pick(l, k):
            return field[jnp.clip(near_cols[l, k] - first, 0, 3 * leaves - 1)]

        near_product(result, 1, near_count, pick, True)

        @pl.when(row > 0)
        def _():
            wait_bytes(coef.at[pl.ds(0, grp)], coef_recv.at[phase, 0])

        @pl.when(row < rows - 1)
        def _():
            wait_bytes(coef.at[pl.ds(0, grp)], coef_recv.at[phase, 2])

        def slot(box):
            return jnp.clip(box - (row * grp - grp), 0, 3 * grp - 1)

        parts = []
        for l in range(leaves):
            taken = jnp.concatenate(
                [
                    coef[slot(lax.div(leaf_far[l, k], leaves)), 0]
                    for k in range(leaf_slots)
                ],
                axis=1,
            )
            parts.append(nt(taken, leaf_weights[l]))
        local = jnp.concatenate(parts, axis=1)
        taken = jnp.concatenate(
            [coef[slot(box_far[0, k]), 1] for k in range(box_slots)], axis=1
        )
        local = local + nt(taken, box_weights[...])
        if rows > 1:
            wait_bytes(group.at[pl.ds(0, rows - 1)], group_recv.at[phase])
        taken = jnp.concatenate([group[coarse_far[0, k]] for k in range(coarse_slots)], axis=1)
        local = local + nt(taken, group_weights[...])
        far = jnp.dot(local.astype(bf16), receive_basis[...], preferred_element_type=f32)
        for l in range(leaves):
            result[l] = result[l] + far[:, l * cells : (l + 1) * cells]

    def drain(phase, field, coef, group):
        own = field.at[pl.ds(leaves, leaves)]

        @pl.when(me < devices - 1)
        def _():
            wait_bytes(own, field_send.at[phase, 0])

        @pl.when(me > 0)
        def _():
            wait_bytes(own, field_send.at[phase, 1])

        @pl.when(row > 0)
        def _():
            wait_bytes(coef.at[pl.ds(0, grp)], coef_send.at[phase, 0])

        if grp > 1:
            wait_bytes(coef.at[pl.ds(0, grp - 1)], coef_send.at[phase, 1])

        @pl.when(row < rows - 1)
        def _():
            wait_bytes(coef.at[pl.ds(0, grp)], coef_send.at[phase, 2])

        if rows > 1:
            wait_bytes(group.at[pl.ds(0, rows - 1)], group_send.at[phase])

    def start_sums(columns):
        spread = jnp.zeros((rhs, LANES), f32)
        for n, column in enumerate(columns):
            spread = jnp.where(lane_at == sub_at + n * rhs, column, spread)
        sums[me] = jnp.sum(spread, axis=0, keepdims=True)

        def send_sums(to_row, to_z):
            send(sums.at[me], sums.at[me], sums_send, sums_recv, to_row, to_z)

        each_other(send_sums)

    def finish_sums(count):
        wait_bytes(sums.at[pl.ds(0, devices - 1)], sums_recv)
        line = jnp.sum(sums[...], axis=0) / total_count
        spread = jnp.broadcast_to(line, (rhs, LANES))
        return [
            jnp.sum(jnp.where(lane_at == sub_at + n * rhs, spread, 0.0), axis=1, keepdims=True)
            for n in range(count)
        ]

    def products(pairs):
        columns = []
        for left, right in pairs:
            total = left[0] * right[0]
            for l in range(1, leaves):
                total = total + left[l] * right[l]
            columns.append(jnp.sum(total, axis=1, keepdims=True))
        return columns

    def first_sums():
        return products([(vector, vector), (vector, image), (image, image)])

    operator(
        0,
        vector,
        image,
        field_a,
        coef_a,
        group_a,
        lambda: [],
        prepare_receive,
        loads[5].wait,
    )
    operator(
        1,
        image,
        image_two,
        field_b,
        coef_b,
        group_b,
        first_sums,
        lambda: None,
        lambda: None,
    )

    together = group_b[0].astype(f32)
    for n in range(1, rows):
        together = together + group_b[n].astype(f32)
    vv, vu, uu = [column / total_count for column in read_sums(together, 3)]
    norm_first = jnp.sqrt(vv + epsilon)
    scale_first = 1.0 / norm_first
    first_square = vv * scale_first * scale_first
    proj_first = (0.5 * vv + vu) * scale_first * scale_first
    shift = 0.5 - proj_first
    image_square = (uu + 2.0 * shift * vu + shift * shift * vv) * scale_first * scale_first
    norm_image = jnp.sqrt(jnp.maximum(image_square, 0.0) + epsilon)
    scale = scale_first / norm_image
    stores = [
        pltpu.make_async_copy(source, result, store_sem.at[n])
        for n, (source, result) in enumerate(
            zip((basis_out, remainder_out, hessenberg_out), results)
        )
    ]
    for l in range(leaves):
        basis = (image[l] + shift * vector[l]) * scale
        basis_out[l] = basis
        remainder_out[l] = 0.5 * basis + (image_two[l] + shift * image[l]) * scale
    start_sums(
        products(
            [
                (vector, remainder_out),
                (basis_out, remainder_out),
                (remainder_out, remainder_out),
                (basis_out, vector),
                (basis_out, basis_out),
            ]
        )
    )
    stores[0].start()
    drain(0, field_a, coef_a, group_a)
    first_with, basis_with, square_two, cross_term, basis_square = finish_sums(5)
    first_with = first_with * scale_first
    cross_term = cross_term * scale_first
    proj_basis = basis_with - first_with * cross_term
    first_part = first_with * scale_first
    for l in range(leaves):
        remainder_out[l] = (
            remainder_out[l] - first_part * vector[l] - proj_basis * basis_out[l]
        )
    stores[1].start()
    last_square = (
        square_two
        + first_with * first_with * first_square
        + proj_basis * proj_basis * basis_square
        - 2.0 * first_with * first_with
        - 2.0 * proj_basis * basis_with
        + 2.0 * first_with * proj_basis * cross_term
    )
    norm_last = jnp.sqrt(jnp.maximum(last_square, 0.0) + epsilon)
    for n, entry in enumerate([proj_first, norm_image, first_with, proj_basis, norm_last]):
        line = jnp.sum(jnp.where(lane_at == sub_at, entry, 0.0), axis=0, keepdims=True)
        hessenberg_out[n : n + 1, :] = line[:, :rhs]
    stores[2].start()
    drain(1, field_b, coef_b, group_b)
    wait_bytes(sums.at[pl.ds(0, devices - 1)], sums_send)
    for store in stores:
        store.wait()


def hand_on(*refs):
    sources, results, places, load_sem, store_sem = refs[:3], refs[3:6], refs[6:9], refs[9], refs[10]
    loads = [pltpu.make_async_copy(sources[n], places[n], load_sem.at[n]) for n in range(3)]
    stores = [pltpu.make_async_copy(places[n], results[n], store_sem.at[n]) for n in range(3)]
    for load in loads:
        load.start()
    for load, store in zip(loads, stores):
        load.wait()
        store.start()
    for store in stores:
        store.wait()


def shards(
    rows,
    grp,
    vector,
    near_cols,
    near_blocks,
    col_basis,
    row_basis,
    leaf_far,
    leaf_coupling,
    leaf_transfer,
    box_far,
    box_coupling,
    box_transfer,
    coarse_far,
    coarse_coupling,
):
    leaves, rhs, cells = vector.shape
    rank = col_basis.shape[1]
    assert leaves * rank == LANES and box_far.shape[0] == 1 and coarse_far.shape[0] == 1
    assert 5 * rhs <= LANES and 2 * rank + 9 <= LANES and rank & (rank - 1) == 0
    hbm = pl.BlockSpec(memory_space=pltpu.HBM)
    slots = max(leaf_far.shape[1], box_far.shape[1], coarse_far.shape[1])
    dma = pltpu.SemaphoreType.DMA
    operands = (
        near_cols,
        leaf_far,
        box_far,
        coarse_far,
        vector,
        near_blocks,
        col_basis,
        row_basis,
        leaf_coupling,
        leaf_transfer,
        box_coupling,
        box_transfer,
        coarse_coupling,
    )
    shapes = (
        jax.ShapeDtypeStruct(vector.shape, f32),
        jax.ShapeDtypeStruct(vector.shape, f32),
        jax.ShapeDtypeStruct((5, rhs), f32),
    )
    results = pl.pallas_call(
        functools.partial(kernel, rows, grp),
        out_shape=shapes,
        in_specs=[hbm] * len(operands),
        out_specs=(hbm, hbm, hbm),
        scratch_shapes=[
            *[pltpu.SMEM(operand.shape, operand.dtype) for operand in operands[:4]],
            *[pltpu.VMEM(operand.shape, operand.dtype) for operand in operands[4:]],
            pltpu.VMEM((3 * leaves, rhs, cells), bf16),
            pltpu.VMEM((3 * leaves, rhs, cells), bf16),
            pltpu.VMEM((3 * grp, 2, rhs, LANES), bf16),
            pltpu.VMEM((3 * grp, 2, rhs, LANES), bf16),
            pltpu.VMEM((rows, rhs, LANES), bf16),
            pltpu.VMEM((rows, rhs, LANES), bf16),
            pltpu.VMEM((rows * grp, 1, LANES), f32),
            pltpu.VMEM((2 * LANES, leaves * cells), bf16),
            pltpu.VMEM((LANES, leaves * cells), bf16),
            pltpu.VMEM((leaves, rank, leaf_far.shape[1] * LANES), bf16),
            pltpu.VMEM((LANES, box_far.shape[1] * LANES), bf16),
            pltpu.VMEM((LANES, coarse_far.shape[1] * LANES), bf16),
            pltpu.VMEM(vector.shape, f32),
            pltpu.VMEM(vector.shape, f32),
            pltpu.VMEM((*near_blocks.shape[:2], leaves * rhs, cells), bf16),
            pltpu.VMEM((slots * rank, slots * LANES), bf16),
            pltpu.VMEM(vector.shape, f32),
            pltpu.VMEM(vector.shape, f32),
            pltpu.VMEM((5, rhs), f32),
            dma((3,)),
            dma((len(operands),)),
            dma((2, 2)),
            dma((2, 2)),
            dma((2, 3)),
            dma((2, 3)),
            dma((2,)),
            dma((2,)),
            dma(()),
            dma(()),
        ],
        compiler_params=pltpu.CompilerParams(
            collective_id=0, has_side_effects=True, vmem_limit_bytes=65100 * 1024
        ),
    )(*operands)
    basis, remainder, entries = pl.pallas_call(
        hand_on,
        out_shape=shapes,
        in_specs=[hbm] * 3,
        out_specs=(hbm, hbm, hbm),
        scratch_shapes=[pltpu.VMEM(shape.shape, f32) for shape in shapes] + [dma((3,))] * 2,
        compiler_params=pltpu.CompilerParams(vmem_limit_bytes=65100 * 1024),
    )(*results)
    return basis, remainder, entries.T


def solution(mesh):
    return jax.shard_map(
        functools.partial(shards, mesh.shape["rows"], mesh.shape["grp"]),
        mesh=mesh,
        in_specs=(
            P(("rows", "grp"), None, None),
            P(("rows", "grp"), None),
            P(("rows", "grp"), None, None, None),
            P(("rows", "grp"), None, None),
            P(("rows", "grp"), None, None),
            P(("rows", "grp"), None),
            P(("rows", "grp"), None, None),
            P(("rows", "grp"), None, None),
            P(("rows", "grp"), None),
            P(("rows", "grp"), None, None),
            P(("rows", "grp"), None, None),
            P("rows", None),
            P("rows", None, None),
        ),
        out_specs=(P(("rows", "grp"), None, None), P(("rows", "grp"), None, None), P()),
        check_vma=False,
    )
```

```python
import functools

import jax
import jax.numpy as jnp
from jax import lax
from jax.experimental import pallas as pl
from jax.experimental.pallas import tpu as pltpu
from jax.sharding import PartitionSpec as P

LANES = 128
epsilon = 1e-06
highest = lax.Precision.HIGHEST
MESH = pl.DeviceIdType.MESH
bf16 = jnp.bfloat16
f32 = jnp.float32


def nt(left, right, precision=None):
    return lax.dot_general(
        left, right, (((1,), (1,)), ((), ())), precision=precision, preferred_element_type=f32
    )


def wrap(index, size):
    return jnp.where(index >= size, index - size, index)


def kernel(
    rows,
    grp,
    *refs,
):
    sources = refs[:13]
    results = refs[13:16]
    targets = refs[16:29]
    (
        near_cols,
        leaf_far,
        box_far,
        coarse_far,
        vector,
        near_blocks,
        col_basis,
        row_basis,
        leaf_coupling,
        leaf_transfer,
        box_coupling,
        box_transfer,
        coarse_coupling,
    ) = targets
    (
        field_a,
        field_b,
        coef_a,
        coef_b,
        group_a,
        group_b,
        sums,
        send_basis,
        receive_basis,
        leaf_weights,
        box_weights,
        group_weights,
        image,
        image_two,
        picked,
        select,
        basis_out,
        remainder_out,
        hessenberg_out,
        store_sem,
        load_sem,
        field_send,
        field_recv,
        coef_send,
        coef_recv,
        group_send,
        group_recv,
        sums_send,
        sums_recv,
    ) = refs[29:]
    leaves, rhs, cells = vector.shape
    rank = col_basis.shape[1]
    near_count = near_cols.shape[1]
    leaf_slots = leaf_far.shape[1]
    box_slots = box_far.shape[1]
    coarse_slots = coarse_far.shape[1]
    devices = rows * grp
    total_count = leaves * devices * cells
    row = lax.axis_index("rows")
    z = lax.axis_index("grp")
    me = row * grp + z

    loads = [
        pltpu.make_async_copy(source, target, load_sem.at[n])
        for n, (source, target) in enumerate(zip(sources, targets))
    ]
    for n in (4, 6, 9, 11, 7, 8, 10, 12, 0, 1, 2, 3, 5):
        loads[n].start()

    barrier = pltpu.get_barrier_semaphore()

    def each_other(visit):
        def one_row(step, carry):
            to_row = wrap(row + step, rows)
            for turn in range(grp):
                visit(to_row, wrap(z + turn, grp))
            return carry

        for turn in range(1, grp):
            visit(row, wrap(z + turn, grp))
        lax.fori_loop(1, rows, one_row, 0)

    def greet(to_row, to_z):
        pl.semaphore_signal(barrier, inc=1, device_id=(to_row, to_z), device_id_type=MESH)

    each_other(greet)

    send_basis[...] = jnp.zeros_like(send_basis)
    picked[...] = jnp.zeros_like(picked)
    for n in (4, 6, 9, 11):
        loads[n].wait()
    for l in range(leaves):
        send_basis[l * rank : (l + 1) * rank, l * cells : (l + 1) * cells] = col_basis[l]
    width = leaves * rank
    transfer = leaf_transfer[...].reshape(width, rank)
    down = jnp.dot(transfer, box_transfer[0], precision=highest, preferred_element_type=f32)
    up = jnp.concatenate([transfer, down, jnp.zeros((width, LANES - 2 * rank), f32)], axis=1)
    up_high = up.astype(bf16)
    up_low = (up - up_high.astype(f32)).astype(bf16)

    def prepare_receive():
        for n in (7, 8, 10, 12, 0, 1, 2, 3):
            loads[n].wait()
        receive_basis[...] = jnp.zeros_like(receive_basis)
        for l in range(leaves):
            receive_basis[l * rank : (l + 1) * rank, l * cells : (l + 1) * cells] = row_basis[l]
        lane = lax.broadcasted_iota(jnp.int32, (rank, LANES), 1)
        unit = lax.broadcasted_iota(jnp.int32, (rank, LANES), 0)
        select[...] = jnp.zeros_like(select)
        for k in range(select.shape[0] // rank):
            select[k * rank : (k + 1) * rank, k * LANES : (k + 1) * LANES] = jnp.where(
                (lane & (rank - 1)) == unit, 1.0, 0.0
            ).astype(bf16)
        tiled = jnp.dot(
            leaf_coupling[...].reshape(width, leaf_slots * rank),
            select[: leaf_slots * rank, : leaf_slots * LANES],
            preferred_element_type=f32,
        )
        for l in range(leaves):
            for k in range(leaf_slots):
                start = lax.rem(leaf_far[l, k], leaves) * rank
                piece = tiled[l * rank : (l + 1) * rank, k * LANES : (k + 1) * LANES]
                leaf_weights[l, :, k * LANES : (k + 1) * LANES] = jnp.where(
                    (lane >= start) & (lane < start + rank), piece, 0.0
                ).astype(bf16)

        def compose(target, coupling, above, low):
            slots = coupling.shape[1] // rank
            wide = jnp.dot(
                coupling, select[: slots * rank, : slots * LANES], preferred_element_type=f32
            )
            place = lax.broadcasted_iota(jnp.int32, wide.shape, 1) & (LANES - 1)
            wide = jnp.where((place >= low) & (place < low + rank), wide, 0.0).astype(bf16)
            above_high = above.astype(bf16)
            above_low = (above - above_high.astype(f32)).astype(bf16)
            target[...] = (
                jnp.dot(above_high, wide, preferred_element_type=f32)
                + jnp.dot(above_low, wide, preferred_element_type=f32)
            ).astype(bf16)

        compose(box_weights, box_coupling[0], transfer, 0)
        compose(group_weights, coarse_coupling[0], down, rank)

    def send(src, dst, send_sem, recv_sem, to_row, to_z):
        pltpu.make_async_remote_copy(
            src_ref=src,
            dst_ref=dst,
            send_sem=send_sem,
            recv_sem=recv_sem,
            device_id=(to_row, to_z),
            device_id_type=MESH,
        ).start()

    def wait_bytes(ref, sem):
        pltpu.make_async_copy(ref, ref, sem).wait()

    def near_product(result, start, stop, pick, add):
        total = None
        for l in range(leaves):
            for k in range(start, stop):
                picked[l, k, l * rhs : (l + 1) * rhs] = pick(l, k)
                product = nt(near_blocks[l, k], picked[l, k])
                total = product if total is None else total + product
        turned = total.T
        for l in range(leaves):
            rows_of = turned[l * rhs : (l + 1) * rhs]
            result[l] = result[l] + rows_of if add else rows_of

    sub_at = lax.broadcasted_iota(jnp.int32, (rhs, LANES), 0)
    lane_at = lax.broadcasted_iota(jnp.int32, (rhs, LANES), 1)

    def with_sums(tile, columns):
        for n, column in enumerate(columns):
            for part in range(3):
                piece = column.astype(bf16).astype(f32)
                tile = jnp.where(lane_at == 2 * rank + 3 * n + part, piece, tile)
                column = column - piece
        return tile

    def read_sums(tile, count):
        return [
            jnp.sum(
                jnp.where(
                    (lane_at >= 2 * rank + 3 * n) & (lane_at < 2 * rank + 3 * n + 3), tile, 0.0
                ),
                axis=1,
                keepdims=True,
            )
            for n in range(count)
        ]

    def operator(phase, source, result, field, coef, group, own_sums, after_send, before_near):
        for l in range(leaves):
            field[leaves + l] = source[l].astype(bf16)
        own = field.at[pl.ds(leaves, leaves)]
        low = field.at[pl.ds(0, leaves)]
        high = field.at[pl.ds(2 * leaves, leaves)]

        wide = jnp.concatenate([field[leaves + l] for l in range(leaves)], axis=1)
        sent = nt(wide, send_basis[...]).astype(bf16)
        mine = grp + z
        coef[mine, 0] = sent
        upward = jnp.dot(sent, up_high, preferred_element_type=f32) + jnp.dot(
            sent, up_low, preferred_element_type=f32
        )
        coef[mine, 1] = with_sums(upward, own_sums()).astype(bf16)
        if phase == 0:
            pl.semaphore_wait(barrier, devices - 1)

        for step in range(1, grp):
            send(
                coef.at[mine],
                coef.at[mine],
                coef_send.at[phase, 1],
                coef_recv.at[phase, 1],
                row,
                wrap(z + step, grp),
            )

        @pl.when(me < devices - 1)
        def _():
            last = z == grp - 1
            send(
                own,
                low,
                field_send.at[phase, 0],
                field_recv.at[phase, 0],
                jnp.where(last, row + 1, row),
                jnp.where(last, 0, z + 1),
            )

        @pl.when(me > 0)
        def _():
            send(
                own,
                high,
                field_send.at[phase, 1],
                field_recv.at[phase, 1],
                jnp.where(z == 0, row - 1, row),
                jnp.where(z == 0, grp - 1, z - 1),
            )

        after_send()
        before_near()
        near_product(result, 0, 1, lambda l, k: field[leaves + l], False)

        if grp > 1:
            wait_bytes(coef.at[pl.ds(0, grp - 1)], coef_recv.at[phase, 1])
        whole_row = coef.at[pl.ds(grp, grp)]

        @pl.when(row > 0)
        def _():
            send(
                whole_row,
                coef.at[pl.ds(2 * grp, grp)],
                coef_send.at[phase, 0],
                coef_recv.at[phase, 2],
                row - 1,
                z,
            )

        @pl.when(row < rows - 1)
        def _():
            send(
                whole_row,
                coef.at[pl.ds(0, grp)],
                coef_send.at[phase, 2],
                coef_recv.at[phase, 0],
                row + 1,
                z,
            )

        together = coef[grp, 1].astype(f32)
        for other in range(1, grp):
            together = together + coef[grp + other, 1].astype(f32)
        if phase == 1:
            together = with_sums(together, read_sums(together, 3))
        group[row] = together.astype(bf16)

        def send_group(step, carry):
            send(
                group.at[row],
                group.at[row],
                group_send.at[phase],
                group_recv.at[phase],
                wrap(row + step, rows),
                z,
            )
            return carry

        lax.fori_loop(1, rows, send_group, 0)

        @pl.when(me > 0)
        def _():
            wait_bytes(low, field_recv.at[phase, 0])

        @pl.when(me < devices - 1)
        def _():
            wait_bytes(high, field_recv.at[phase, 1])

        first = me * leaves - leaves

        def pick(l, k):
            return field[jnp.clip(near_cols[l, k] - first, 0, 3 * leaves - 1)]

        near_product(result, 1, near_count, pick, True)

        @pl.when(row > 0)
        def _():
            wait_bytes(coef.at[pl.ds(0, grp)], coef_recv.at[phase, 0])

        @pl.when(row < rows - 1)
        def _():
            wait_bytes(coef.at[pl.ds(0, grp)], coef_recv.at[phase, 2])

        def slot(box):
            return jnp.clip(box - (row * grp - grp), 0, 3 * grp - 1)

        parts = []
        for l in range(leaves):
            taken = jnp.concatenate(
                [
                    coef[slot(lax.div(leaf_far[l, k], leaves)), 0]
                    for k in range(leaf_slots)
                ],
                axis=1,
            )
            parts.append(nt(taken, leaf_weights[l]))
        local = jnp.concatenate(parts, axis=1)
        taken = jnp.concatenate(
            [coef[slot(box_far[0, k]), 1] for k in range(box_slots)], axis=1
        )
        local = local + nt(taken, box_weights[...])
        if rows > 1:
            wait_bytes(group.at[pl.ds(0, rows - 1)], group_recv.at[phase])
        taken = jnp.concatenate([group[coarse_far[0, k]] for k in range(coarse_slots)], axis=1)
        local = local + nt(taken, group_weights[...])
        far = jnp.dot(local.astype(bf16), receive_basis[...], preferred_element_type=f32)
        for l in range(leaves):
            result[l] = result[l] + far[:, l * cells : (l + 1) * cells]

    def drain(phase, field, coef, group):
        own = field.at[pl.ds(leaves, leaves)]

        @pl.when(me < devices - 1)
        def _():
            wait_bytes(own, field_send.at[phase, 0])

        @pl.when(me > 0)
        def _():
            wait_bytes(own, field_send.at[phase, 1])

        @pl.when(row > 0)
        def _():
            wait_bytes(coef.at[pl.ds(0, grp)], coef_send.at[phase, 0])

        if grp > 1:
            wait_bytes(coef.at[pl.ds(0, grp - 1)], coef_send.at[phase, 1])

        @pl.when(row < rows - 1)
        def _():
            wait_bytes(coef.at[pl.ds(0, grp)], coef_send.at[phase, 2])

        if rows > 1:
            wait_bytes(group.at[pl.ds(0, rows - 1)], group_send.at[phase])

    def start_sums(columns):
        spread = jnp.zeros((rhs, LANES), f32)
        for n, column in enumerate(columns):
            spread = jnp.where(lane_at == sub_at + n * rhs, column, spread)
        sums[me] = jnp.sum(spread, axis=0, keepdims=True)

        def send_sums(to_row, to_z):
            send(sums.at[me], sums.at[me], sums_send, sums_recv, to_row, to_z)

        each_other(send_sums)

    def finish_sums(count):
        wait_bytes(sums.at[pl.ds(0, devices - 1)], sums_recv)
        line = jnp.sum(sums[...], axis=0) / total_count
        spread = jnp.broadcast_to(line, (rhs, LANES))
        return [
            jnp.sum(jnp.where(lane_at == sub_at + n * rhs, spread, 0.0), axis=1, keepdims=True)
            for n in range(count)
        ]

    def products(pairs):
        columns = []
        for left, right in pairs:
            total = left[0] * right[0]
            for l in range(1, leaves):
                total = total + left[l] * right[l]
            columns.append(jnp.sum(total, axis=1, keepdims=True))
        return columns

    def first_sums():
        return products([(vector, vector), (vector, image), (image, image)])

    operator(
        0,
        vector,
        image,
        field_a,
        coef_a,
        group_a,
        lambda: [],
        prepare_receive,
        loads[5].wait,
    )
    operator(
        1,
        image,
        image_two,
        field_b,
        coef_b,
        group_b,
        first_sums,
        lambda: None,
        lambda: None,
    )

    together = group_b[0].astype(f32)
    for n in range(1, rows):
        together = together + group_b[n].astype(f32)
    vv, vu, uu = [column / total_count for column in read_sums(together, 3)]
    norm_first = jnp.sqrt(vv + epsilon)
    scale_first = 1.0 / norm_first
    first_square = vv * scale_first * scale_first
    proj_first = (0.5 * vv + vu) * scale_first * scale_first
    shift = 0.5 - proj_first
    image_square = (uu + 2.0 * shift * vu + shift * shift * vv) * scale_first * scale_first
    norm_image = jnp.sqrt(jnp.maximum(image_square, 0.0) + epsilon)
    scale = scale_first / norm_image
    stores = [
        pltpu.make_async_copy(source, result, store_sem.at[n])
        for n, (source, result) in enumerate(
            zip((basis_out, remainder_out, hessenberg_out), results)
        )
    ]
    for l in range(leaves):
        basis = (image[l] + shift * vector[l]) * scale
        basis_out[l] = basis
        remainder_out[l] = 0.5 * basis + (image_two[l] + shift * image[l]) * scale
    start_sums(
        products(
            [
                (vector, remainder_out),
                (basis_out, remainder_out),
                (remainder_out, remainder_out),
                (basis_out, vector),
                (basis_out, basis_out),
            ]
        )
    )
    stores[0].start()
    drain(0, field_a, coef_a, group_a)
    first_with, basis_with, square_two, cross_term, basis_square = finish_sums(5)
    first_with = first_with * scale_first
    cross_term = cross_term * scale_first
    proj_basis = basis_with - first_with * cross_term
    first_part = first_with * scale_first
    for l in range(leaves):
        remainder_out[l] = (
            remainder_out[l] - first_part * vector[l] - proj_basis * basis_out[l]
        )
    stores[1].start()
    last_square = (
        square_two
        + first_with * first_with * first_square
        + proj_basis * proj_basis * basis_square
        - 2.0 * first_with * first_with
        - 2.0 * proj_basis * basis_with
        + 2.0 * first_with * proj_basis * cross_term
    )
    norm_last = jnp.sqrt(jnp.maximum(last_square, 0.0) + epsilon)
    for n, entry in enumerate([proj_first, norm_image, first_with, proj_basis, norm_last]):
        line = jnp.sum(jnp.where(lane_at == sub_at, entry, 0.0), axis=0, keepdims=True)
        hessenberg_out[n : n + 1, :] = line[:, :rhs]
    stores[2].start()
    drain(1, field_b, coef_b, group_b)
    wait_bytes(sums.at[pl.ds(0, devices - 1)], sums_send)
    for store in stores:
        store.wait()


def hand_on(*refs):
    sources, results, places, load_sem, store_sem = refs[:3], refs[3:6], refs[6:9], refs[9], refs[10]
    loads = [pltpu.make_async_copy(sources[n], places[n], load_sem.at[n]) for n in range(3)]
    stores = [pltpu.make_async_copy(places[n], results[n], store_sem.at[n]) for n in range(3)]
    for load in loads:
        load.start()
    for load, store in zip(loads, stores):
        load.wait()
        store.start()
    for store in stores:
        store.wait()


def shards(
    rows,
    grp,
    vector,
    near_cols,
    near_blocks,
    col_basis,
    row_basis,
    leaf_far,
    leaf_coupling,
    leaf_transfer,
    box_far,
    box_coupling,
    box_transfer,
    coarse_far,
    coarse_coupling,
):
    leaves, rhs, cells = vector.shape
    rank = col_basis.shape[1]
    assert leaves * rank == LANES and box_far.shape[0] == 1 and coarse_far.shape[0] == 1
    assert 5 * rhs <= LANES and 2 * rank + 9 <= LANES and rank & (rank - 1) == 0
    hbm = pl.BlockSpec(memory_space=pltpu.HBM)
    slots = max(leaf_far.shape[1], box_far.shape[1], coarse_far.shape[1])
    dma = pltpu.SemaphoreType.DMA
    operands = (
        near_cols,
        leaf_far,
        box_far,
        coarse_far,
        vector,
        near_blocks,
        col_basis,
        row_basis,
        leaf_coupling,
        leaf_transfer,
        box_coupling,
        box_transfer,
        coarse_coupling,
    )
    shapes = (
        jax.ShapeDtypeStruct(vector.shape, f32),
        jax.ShapeDtypeStruct(vector.shape, f32),
        jax.ShapeDtypeStruct((5, rhs), f32),
    )
    results = pl.pallas_call(
        functools.partial(kernel, rows, grp),
        out_shape=shapes,
        in_specs=[hbm] * len(operands),
        out_specs=(hbm, hbm, hbm),
        scratch_shapes=[
            *[pltpu.SMEM(operand.shape, operand.dtype) for operand in operands[:4]],
            *[pltpu.VMEM(operand.shape, operand.dtype) for operand in operands[4:]],
            pltpu.VMEM((3 * leaves, rhs, cells), bf16),
            pltpu.VMEM((3 * leaves, rhs, cells), bf16),
            pltpu.VMEM((3 * grp, 2, rhs, LANES), bf16),
            pltpu.VMEM((3 * grp, 2, rhs, LANES), bf16),
            pltpu.VMEM((rows, rhs, LANES), bf16),
            pltpu.VMEM((rows, rhs, LANES), bf16),
            pltpu.VMEM((rows * grp, 1, LANES), f32),
            pltpu.VMEM((LANES, leaves * cells), bf16),
            pltpu.VMEM((LANES, leaves * cells), bf16),
            pltpu.VMEM((leaves, rank, leaf_far.shape[1] * LANES), bf16),
            pltpu.VMEM((LANES, box_far.shape[1] * LANES), bf16),
            pltpu.VMEM((LANES, coarse_far.shape[1] * LANES), bf16),
            pltpu.VMEM(vector.shape, f32),
            pltpu.VMEM(vector.shape, f32),
            pltpu.VMEM((*near_blocks.shape[:2], leaves * rhs, cells), bf16),
            pltpu.VMEM((slots * rank, slots * LANES), bf16),
            pltpu.VMEM(vector.shape, f32),
            pltpu.VMEM(vector.shape, f32),
            pltpu.VMEM((5, rhs), f32),
            dma((3,)),
            dma((len(operands),)),
            dma((2, 2)),
            dma((2, 2)),
            dma((2, 3)),
            dma((2, 3)),
            dma((2,)),
            dma((2,)),
            dma(()),
            dma(()),
        ],
        compiler_params=pltpu.CompilerParams(
            collective_id=0, has_side_effects=True, vmem_limit_bytes=65100 * 1024
        ),
    )(*operands)
    basis, remainder, entries = pl.pallas_call(
        hand_on,
        out_shape=shapes,
        in_specs=[hbm] * 3,
        out_specs=(hbm, hbm, hbm),
        scratch_shapes=[pltpu.VMEM(shape.shape, f32) for shape in shapes] + [dma((3,))] * 2,
        compiler_params=pltpu.CompilerParams(vmem_limit_bytes=65100 * 1024),
    )(*results)
    return basis, remainder, entries.T


def solution(mesh):
    return jax.shard_map(
        functools.partial(shards, mesh.shape["rows"], mesh.shape["grp"]),
        mesh=mesh,
        in_specs=(
            P(("rows", "grp"), None, None),
            P(("rows", "grp"), None),
            P(("rows", "grp"), None, None, None),
            P(("rows", "grp"), None, None),
            P(("rows", "grp"), None, None),
            P(("rows", "grp"), None),
            P(("rows", "grp"), None, None),
            P(("rows", "grp"), None, None),
            P(("rows", "grp"), None),
            P(("rows", "grp"), None, None),
            P(("rows", "grp"), None, None),
            P("rows", None),
            P("rows", None, None),
        ),
        out_specs=(P(("rows", "grp"), None, None), P(("rows", "grp"), None, None), P()),
        check_vma=False,
    )
```

```python
import functools

import jax
import jax.numpy as jnp
from jax import lax
from jax.experimental import pallas as pl
from jax.experimental.pallas import tpu as pltpu
from jax.sharding import PartitionSpec as P

LANES = 128
epsilon = 1e-06
highest = lax.Precision.HIGHEST
MESH = pl.DeviceIdType.MESH
bf16 = jnp.bfloat16
f32 = jnp.float32


def nt(left, right, precision=None):
    return lax.dot_general(
        left, right, (((1,), (1,)), ((), ())), precision=precision, preferred_element_type=f32
    )


def wrap(index, size):
    return jnp.where(index >= size, index - size, index)


def kernel(
    rows,
    grp,
    *refs,
):
    sources = refs[:13]
    results = refs[13:16]
    targets = refs[16:29]
    (
        near_cols,
        leaf_far,
        box_far,
        coarse_far,
        vector,
        near_blocks,
        col_basis,
        row_basis,
        leaf_coupling,
        leaf_transfer,
        box_coupling,
        box_transfer,
        coarse_coupling,
    ) = targets
    (
        field_a,
        field_b,
        coef_a,
        coef_b,
        group_a,
        group_b,
        sums,
        send_basis,
        receive_basis,
        leaf_weights,
        box_weights,
        group_weights,
        image,
        image_two,
        picked,
        select,
        basis_out,
        remainder_out,
        hessenberg_out,
        store_sem,
        load_sem,
        field_send,
        field_recv,
        coef_send,
        coef_recv,
        group_send,
        group_recv,
        sums_send,
        sums_recv,
    ) = refs[29:]
    leaves, rhs, cells = vector.shape
    rank = col_basis.shape[1]
    near_count = near_cols.shape[1]
    leaf_slots = leaf_far.shape[1]
    box_slots = box_far.shape[1]
    coarse_slots = coarse_far.shape[1]
    devices = rows * grp
    total_count = leaves * devices * cells
    row = lax.axis_index("rows")
    z = lax.axis_index("grp")
    me = row * grp + z

    loads = [
        pltpu.make_async_copy(source, target, load_sem.at[n])
        for n, (source, target) in enumerate(zip(sources, targets))
    ]
    for n in (4, 6, 9, 11, 7, 8, 10, 12, 0, 1, 2, 3, 5):
        loads[n].start()

    barrier = pltpu.get_barrier_semaphore()

    def each_other(visit):
        def one_row(step, carry):
            to_row = wrap(row + step, rows)
            for turn in range(grp):
                visit(to_row, wrap(z + turn, grp))
            return carry

        for turn in range(1, grp):
            visit(row, wrap(z + turn, grp))
        lax.fori_loop(1, rows, one_row, 0)

    def greet(to_row, to_z):
        pl.semaphore_signal(barrier, inc=1, device_id=(to_row, to_z), device_id_type=MESH)

    each_other(greet)

    send_basis[...] = jnp.zeros_like(send_basis)
    picked[...] = jnp.zeros_like(picked)
    for n in (4, 6, 9, 11):
        loads[n].wait()
    for l in range(leaves):
        send_basis[l * rank : (l + 1) * rank, l * cells : (l + 1) * cells] = col_basis[l]
    width = leaves * rank
    transfer = leaf_transfer[...].reshape(width, rank)
    down = jnp.dot(transfer, box_transfer[0], precision=highest, preferred_element_type=f32)
    up = jnp.concatenate([transfer, down, jnp.zeros((width, LANES - 2 * rank), f32)], axis=1)
    up_high = up.astype(bf16)
    up_low = (up - up_high.astype(f32)).astype(bf16)

    def prepare_receive():
        for n in (7, 8, 10, 12, 0, 1, 2, 3):
            loads[n].wait()
        receive_basis[...] = jnp.zeros_like(receive_basis)
        for l in range(leaves):
            receive_basis[l * rank : (l + 1) * rank, l * cells : (l + 1) * cells] = row_basis[l]
        lane = lax.broadcasted_iota(jnp.int32, (rank, LANES), 1)
        unit = lax.broadcasted_iota(jnp.int32, (rank, LANES), 0)
        select[...] = jnp.zeros_like(select)
        for k in range(select.shape[0] // rank):
            select[k * rank : (k + 1) * rank, k * LANES : (k + 1) * LANES] = jnp.where(
                (lane & (rank - 1)) == unit, 1.0, 0.0
            ).astype(bf16)
        tiled = jnp.dot(
            leaf_coupling[...].reshape(width, leaf_slots * rank),
            select[: leaf_slots * rank, : leaf_slots * LANES],
            preferred_element_type=f32,
        )
        for l in range(leaves):
            for k in range(leaf_slots):
                start = lax.rem(leaf_far[l, k], leaves) * rank
                piece = tiled[l * rank : (l + 1) * rank, k * LANES : (k + 1) * LANES]
                leaf_weights[l, :, k * LANES : (k + 1) * LANES] = jnp.where(
                    (lane >= start) & (lane < start + rank), piece, 0.0
                ).astype(bf16)

        def compose(target, coupling, above, low):
            slots = coupling.shape[1] // rank
            wide = jnp.dot(
                coupling, select[: slots * rank, : slots * LANES], preferred_element_type=f32
            )
            place = lax.broadcasted_iota(jnp.int32, wide.shape, 1) & (LANES - 1)
            wide = jnp.where((place >= low) & (place < low + rank), wide, 0.0).astype(bf16)
            above_high = above.astype(bf16)
            above_low = (above - above_high.astype(f32)).astype(bf16)
            target[...] = (
                jnp.dot(above_high, wide, preferred_element_type=f32)
                + jnp.dot(above_low, wide, preferred_element_type=f32)
            ).astype(bf16)

        compose(box_weights, box_coupling[0], transfer, 0)
        compose(group_weights, coarse_coupling[0], down, rank)

    def send(src, dst, send_sem, recv_sem, to_row, to_z):
        pltpu.make_async_remote_copy(
            src_ref=src,
            dst_ref=dst,
            send_sem=send_sem,
            recv_sem=recv_sem,
            device_id=(to_row, to_z),
            device_id_type=MESH,
        ).start()

    def wait_bytes(ref, sem):
        pltpu.make_async_copy(ref, ref, sem).wait()

    def near_product(result, start, stop, pick, add):
        total = None
        for l in range(leaves):
            for k in range(start, stop):
                picked[l, k, l * rhs : (l + 1) * rhs] = pick(l, k)
                product = nt(near_blocks[l, k], picked[l, k])
                total = product if total is None else total + product
        turned = total.T
        for l in range(leaves):
            rows_of = turned[l * rhs : (l + 1) * rhs]
            result[l] = result[l] + rows_of if add else rows_of

    sub_at = lax.broadcasted_iota(jnp.int32, (rhs, LANES), 0)
    lane_at = lax.broadcasted_iota(jnp.int32, (rhs, LANES), 1)

    def with_sums(tile, columns):
        for n, column in enumerate(columns):
            for part in range(3):
                piece = column.astype(bf16).astype(f32)
                tile = jnp.where(lane_at == 2 * rank + 3 * n + part, piece, tile)
                column = column - piece
        return tile

    def read_sums(tile, count):
        return [
            jnp.sum(
                jnp.where(
                    (lane_at >= 2 * rank + 3 * n) & (lane_at < 2 * rank + 3 * n + 3), tile, 0.0
                ),
                axis=1,
                keepdims=True,
            )
            for n in range(count)
        ]

    def operator(phase, source, result, field, coef, group, own_sums, after_send, before_near):
        for l in range(leaves):
            field[leaves + l] = source[l].astype(bf16)
        own = field.at[pl.ds(leaves, leaves)]
        low = field.at[pl.ds(0, leaves)]
        high = field.at[pl.ds(2 * leaves, leaves)]

        wide = jnp.concatenate([field[leaves + l] for l in range(leaves)], axis=1)
        sent = nt(wide, send_basis[...]).astype(bf16)
        mine = grp + z
        coef[mine, 0] = sent
        upward = jnp.dot(sent, up_high, preferred_element_type=f32) + jnp.dot(
            sent, up_low, preferred_element_type=f32
        )
        coef[mine, 1] = with_sums(upward, own_sums()).astype(bf16)
        if phase == 0:
            pl.semaphore_wait(barrier, devices - 1)

        for step in range(1, grp):
            send(
                coef.at[mine],
                coef.at[mine],
                coef_send.at[phase, 1],
                coef_recv.at[phase, 1],
                row,
                wrap(z + step, grp),
            )

        @pl.when(me < devices - 1)
        def _():
            last = z == grp - 1
            send(
                own,
                low,
                field_send.at[phase, 0],
                field_recv.at[phase, 0],
                jnp.where(last, row + 1, row),
                jnp.where(last, 0, z + 1),
            )

        @pl.when(me > 0)
        def _():
            send(
                own,
                high,
                field_send.at[phase, 1],
                field_recv.at[phase, 1],
                jnp.where(z == 0, row - 1, row),
                jnp.where(z == 0, grp - 1, z - 1),
            )

        before_near()
        near_product(result, 0, 1, lambda l, k: field[leaves + l], False)

        if grp > 1:
            wait_bytes(coef.at[pl.ds(0, grp - 1)], coef_recv.at[phase, 1])
        whole_row = coef.at[pl.ds(grp, grp)]

        @pl.when(row > 0)
        def _():
            send(
                whole_row,
                coef.at[pl.ds(2 * grp, grp)],
                coef_send.at[phase, 0],
                coef_recv.at[phase, 2],
                row - 1,
                z,
            )

        @pl.when(row < rows - 1)
        def _():
            send(
                whole_row,
                coef.at[pl.ds(0, grp)],
                coef_send.at[phase, 2],
                coef_recv.at[phase, 0],
                row + 1,
                z,
            )

        together = coef[grp, 1].astype(f32)
        for other in range(1, grp):
            together = together + coef[grp + other, 1].astype(f32)
        if phase == 1:
            together = with_sums(together, read_sums(together, 3))
        group[row] = together.astype(bf16)

        def send_group(step, carry):
            send(
                group.at[row],
                group.at[row],
                group_send.at[phase],
                group_recv.at[phase],
                wrap(row + step, rows),
                z,
            )
            return carry

        lax.fori_loop(1, rows, send_group, 0)
        after_send()

        @pl.when(me > 0)
        def _():
            wait_bytes(low, field_recv.at[phase, 0])

        @pl.when(me < devices - 1)
        def _():
            wait_bytes(high, field_recv.at[phase, 1])

        first = me * leaves - leaves

        def pick(l, k):
            return field[jnp.clip(near_cols[l, k] - first, 0, 3 * leaves - 1)]

        near_product(result, 1, near_count, pick, True)

        @pl.when(row > 0)
        def _():
            wait_bytes(coef.at[pl.ds(0, grp)], coef_recv.at[phase, 0])

        @pl.when(row < rows - 1)
        def _():
            wait_bytes(coef.at[pl.ds(0, grp)], coef_recv.at[phase, 2])

        def slot(box):
            return jnp.clip(box - (row * grp - grp), 0, 3 * grp - 1)

        parts = []
        for l in range(leaves):
            taken = jnp.concatenate(
                [
                    coef[slot(lax.div(leaf_far[l, k], leaves)), 0]
                    for k in range(leaf_slots)
                ],
                axis=1,
            )
            parts.append(nt(taken, leaf_weights[l]))
        local = jnp.concatenate(parts, axis=1)
        taken = jnp.concatenate(
            [coef[slot(box_far[0, k]), 1] for k in range(box_slots)], axis=1
        )
        local = local + nt(taken, box_weights[...])
        if rows > 1:
            wait_bytes(group.at[pl.ds(0, rows - 1)], group_recv.at[phase])
        taken = jnp.concatenate([group[coarse_far[0, k]] for k in range(coarse_slots)], axis=1)
        local = local + nt(taken, group_weights[...])
        far = jnp.dot(local.astype(bf16), receive_basis[...], preferred_element_type=f32)
        for l in range(leaves):
            result[l] = result[l] + far[:, l * cells : (l + 1) * cells]

    def drain(phase, field, coef, group):
        own = field.at[pl.ds(leaves, leaves)]

        @pl.when(me < devices - 1)
        def _():
            wait_bytes(own, field_send.at[phase, 0])

        @pl.when(me > 0)
        def _():
            wait_bytes(own, field_send.at[phase, 1])

        @pl.when(row > 0)
        def _():
            wait_bytes(coef.at[pl.ds(0, grp)], coef_send.at[phase, 0])

        if grp > 1:
            wait_bytes(coef.at[pl.ds(0, grp - 1)], coef_send.at[phase, 1])

        @pl.when(row < rows - 1)
        def _():
            wait_bytes(coef.at[pl.ds(0, grp)], coef_send.at[phase, 2])

        if rows > 1:
            wait_bytes(group.at[pl.ds(0, rows - 1)], group_send.at[phase])

    def start_sums(columns):
        spread = jnp.zeros((rhs, LANES), f32)
        for n, column in enumerate(columns):
            spread = jnp.where(lane_at == sub_at + n * rhs, column, spread)
        sums[me] = jnp.sum(spread, axis=0, keepdims=True)

        def send_sums(to_row, to_z):
            send(sums.at[me], sums.at[me], sums_send, sums_recv, to_row, to_z)

        each_other(send_sums)

    def finish_sums(count):
        wait_bytes(sums.at[pl.ds(0, devices - 1)], sums_recv)
        line = jnp.sum(sums[...], axis=0) / total_count
        spread = jnp.broadcast_to(line, (rhs, LANES))
        return [
            jnp.sum(jnp.where(lane_at == sub_at + n * rhs, spread, 0.0), axis=1, keepdims=True)
            for n in range(count)
        ]

    def products(pairs):
        columns = []
        for left, right in pairs:
            total = left[0] * right[0]
            for l in range(1, leaves):
                total = total + left[l] * right[l]
            columns.append(jnp.sum(total, axis=1, keepdims=True))
        return columns

    def first_sums():
        return products([(vector, vector), (vector, image), (image, image)])

    operator(
        0,
        vector,
        image,
        field_a,
        coef_a,
        group_a,
        lambda: [],
        prepare_receive,
        loads[5].wait,
    )
    operator(
        1,
        image,
        image_two,
        field_b,
        coef_b,
        group_b,
        first_sums,
        lambda: None,
        lambda: None,
    )

    together = group_b[0].astype(f32)
    for n in range(1, rows):
        together = together + group_b[n].astype(f32)
    vv, vu, uu = [column / total_count for column in read_sums(together, 3)]
    norm_first = jnp.sqrt(vv + epsilon)
    scale_first = 1.0 / norm_first
    first_square = vv * scale_first * scale_first
    proj_first = (0.5 * vv + vu) * scale_first * scale_first
    shift = 0.5 - proj_first
    image_square = (uu + 2.0 * shift * vu + shift * shift * vv) * scale_first * scale_first
    norm_image = jnp.sqrt(jnp.maximum(image_square, 0.0) + epsilon)
    scale = scale_first / norm_image
    stores = [
        pltpu.make_async_copy(source, result, store_sem.at[n])
        for n, (source, result) in enumerate(
            zip((basis_out, remainder_out, hessenberg_out), results)
        )
    ]
    for l in range(leaves):
        basis = (image[l] + shift * vector[l]) * scale
        basis_out[l] = basis
        remainder_out[l] = 0.5 * basis + (image_two[l] + shift * image[l]) * scale
    start_sums(
        products(
            [
                (vector, remainder_out),
                (basis_out, remainder_out),
                (remainder_out, remainder_out),
                (basis_out, vector),
                (basis_out, basis_out),
            ]
        )
    )
    stores[0].start()
    drain(0, field_a, coef_a, group_a)
    first_with, basis_with, square_two, cross_term, basis_square = finish_sums(5)
    first_with = first_with * scale_first
    cross_term = cross_term * scale_first
    proj_basis = basis_with - first_with * cross_term
    first_part = first_with * scale_first
    for l in range(leaves):
        remainder_out[l] = (
            remainder_out[l] - first_part * vector[l] - proj_basis * basis_out[l]
        )
    stores[1].start()
    last_square = (
        square_two
        + first_with * first_with * first_square
        + proj_basis * proj_basis * basis_square
        - 2.0 * first_with * first_with
        - 2.0 * proj_basis * basis_with
        + 2.0 * first_with * proj_basis * cross_term
    )
    norm_last = jnp.sqrt(jnp.maximum(last_square, 0.0) + epsilon)
    for n, entry in enumerate([proj_first, norm_image, first_with, proj_basis, norm_last]):
        line = jnp.sum(jnp.where(lane_at == sub_at, entry, 0.0), axis=0, keepdims=True)
        hessenberg_out[n : n + 1, :] = line[:, :rhs]
    stores[2].start()
    drain(1, field_b, coef_b, group_b)
    wait_bytes(sums.at[pl.ds(0, devices - 1)], sums_send)
    for store in stores:
        store.wait()


def hand_on(*refs):
    sources, results, places, load_sem, store_sem = refs[:3], refs[3:6], refs[6:9], refs[9], refs[10]
    loads = [pltpu.make_async_copy(sources[n], places[n], load_sem.at[n]) for n in range(3)]
    stores = [pltpu.make_async_copy(places[n], results[n], store_sem.at[n]) for n in range(3)]
    for load in loads:
        load.start()
    for load, store in zip(loads, stores):
        load.wait()
        store.start()
    for store in stores:
        store.wait()


def shards(
    rows,
    grp,
    vector,
    near_cols,
    near_blocks,
    col_basis,
    row_basis,
    leaf_far,
    leaf_coupling,
    leaf_transfer,
    box_far,
    box_coupling,
    box_transfer,
    coarse_far,
    coarse_coupling,
):
    leaves, rhs, cells = vector.shape
    rank = col_basis.shape[1]
    assert leaves * rank == LANES and box_far.shape[0] == 1 and coarse_far.shape[0] == 1
    assert 5 * rhs <= LANES and 2 * rank + 9 <= LANES and rank & (rank - 1) == 0
    hbm = pl.BlockSpec(memory_space=pltpu.HBM)
    slots = max(leaf_far.shape[1], box_far.shape[1], coarse_far.shape[1])
    dma = pltpu.SemaphoreType.DMA
    operands = (
        near_cols,
        leaf_far,
        box_far,
        coarse_far,
        vector,
        near_blocks,
        col_basis,
        row_basis,
        leaf_coupling,
        leaf_transfer,
        box_coupling,
        box_transfer,
        coarse_coupling,
    )
    shapes = (
        jax.ShapeDtypeStruct(vector.shape, f32),
        jax.ShapeDtypeStruct(vector.shape, f32),
        jax.ShapeDtypeStruct((5, rhs), f32),
    )
    results = pl.pallas_call(
        functools.partial(kernel, rows, grp),
        out_shape=shapes,
        in_specs=[hbm] * len(operands),
        out_specs=(hbm, hbm, hbm),
        scratch_shapes=[
            *[pltpu.SMEM(operand.shape, operand.dtype) for operand in operands[:4]],
            *[pltpu.VMEM(operand.shape, operand.dtype) for operand in operands[4:]],
            pltpu.VMEM((3 * leaves, rhs, cells), bf16),
            pltpu.VMEM((3 * leaves, rhs, cells), bf16),
            pltpu.VMEM((3 * grp, 2, rhs, LANES), bf16),
            pltpu.VMEM((3 * grp, 2, rhs, LANES), bf16),
            pltpu.VMEM((rows, rhs, LANES), bf16),
            pltpu.VMEM((rows, rhs, LANES), bf16),
            pltpu.VMEM((rows * grp, 1, LANES), f32),
            pltpu.VMEM((LANES, leaves * cells), bf16),
            pltpu.VMEM((LANES, leaves * cells), bf16),
            pltpu.VMEM((leaves, rank, leaf_far.shape[1] * LANES), bf16),
            pltpu.VMEM((LANES, box_far.shape[1] * LANES), bf16),
            pltpu.VMEM((LANES, coarse_far.shape[1] * LANES), bf16),
            pltpu.VMEM(vector.shape, f32),
            pltpu.VMEM(vector.shape, f32),
            pltpu.VMEM((*near_blocks.shape[:2], leaves * rhs, cells), bf16),
            pltpu.VMEM((slots * rank, slots * LANES), bf16),
            pltpu.VMEM(vector.shape, f32),
            pltpu.VMEM(vector.shape, f32),
            pltpu.VMEM((5, rhs), f32),
            dma((3,)),
            dma((len(operands),)),
            dma((2, 2)),
            dma((2, 2)),
            dma((2, 3)),
            dma((2, 3)),
            dma((2,)),
            dma((2,)),
            dma(()),
            dma(()),
        ],
        compiler_params=pltpu.CompilerParams(
            collective_id=0, has_side_effects=True, vmem_limit_bytes=65100 * 1024
        ),
    )(*operands)
    basis, remainder, entries = pl.pallas_call(
        hand_on,
        out_shape=shapes,
        in_specs=[hbm] * 3,
        out_specs=(hbm, hbm, hbm),
        scratch_shapes=[pltpu.VMEM(shape.shape, f32) for shape in shapes] + [dma((3,))] * 2,
        compiler_params=pltpu.CompilerParams(vmem_limit_bytes=65100 * 1024),
    )(*results)
    return basis, remainder, entries.T


def solution(mesh):
    return jax.shard_map(
        functools.partial(shards, mesh.shape["rows"], mesh.shape["grp"]),
        mesh=mesh,
        in_specs=(
            P(("rows", "grp"), None, None),
            P(("rows", "grp"), None),
            P(("rows", "grp"), None, None, None),
            P(("rows", "grp"), None, None),
            P(("rows", "grp"), None, None),
            P(("rows", "grp"), None),
            P(("rows", "grp"), None, None),
            P(("rows", "grp"), None, None),
            P(("rows", "grp"), None),
            P(("rows", "grp"), None, None),
            P(("rows", "grp"), None, None),
            P("rows", None),
            P("rows", None, None),
        ),
        out_specs=(P(("rows", "grp"), None, None), P(("rows", "grp"), None, None), P()),
        check_vma=False,
    )
```
